256 devices in a mesh: ctx: 64 (over x, z, core), head: 4 (over y).
Axes of the slice: x: 4, y: 4, z: 8, core: 2. Of those that a mesh axis runs over, the one named last changes fastest.
Arguments:
- conv_in: bfloat16 [32768, 2048], P('ctx', 'head'), may hold values from -6 to 6
- conv_weight: float32 [4, 2048], P(None, 'head'), may hold values from -3 to 3
- conv_bias: float32 [2048], P('head'), may hold values from -3 to 3
- qk_weight: bfloat16 [2, 8, 256, 256], P(None, 'head'), may hold values from -0.375 to 0.375
- value_in: bfloat16 [32768, 4096], P('ctx', 'head'), may hold values from -6 to 6
- gate_pre: float32 [2, 8, 32768], P(None, 'head', 'ctx'), may hold values from -6 to 300, as said below
- norm_gain: float32 [4096], P('head'), may hold values from 0.5 to 1.5
- out_weight: bfloat16 [4096, 4096], P('head'), may hold values from -0.125 to 0.125
Outputs:
- layer_out: bfloat16 [32768, 4096], P('ctx', 'head')
The draws below stay inside these ranges and needn't reach their ends.
Inputs may be any that keep to these rules, and one draw needn't show every extreme that they name: gate_pre[0] holds input-gate preactivations and gate_pre[1] forget-gate preactivations.
All inputs are finite; a program needn't handle non-finite values.
Results may differ from the reference program's by a relative error of at most 0.02.
Values may be sent and summed in bfloat16 or wider, within the bound.
A program may use at most 192 MiB of HBM per device.

```python
import math
import jax
import jax.numpy as jnp
from jax import lax

D = 4096
HEAD_TOTAL = 8
DK = 256
DV = 512
CONV = 4
BLOCK = 512
TOK_DEV = 512
TOKEN_TOTAL = 32768
N_HEAD = 4


def draw_gate_pre(key, part):
    key_sequence = jax.random.split(key, 11)
    token_positions = jnp.arange(TOKEN_TOTAL)
    in_gate = jnp.clip(jax.random.normal(key_sequence[0], (HEAD_TOTAL, TOKEN_TOTAL), jnp.float32), -4.0, 4.0)
    slow_count = jax.random.randint(key_sequence[4], (), 3, 6)
    ranking = jax.random.permutation(key_sequence[5], HEAD_TOTAL)
    slow_heads = ranking < slow_count
    rough = jnp.exp(jax.random.uniform(key_sequence[6], (HEAD_TOTAL, TOKEN_TOTAL), jnp.float32, math.log(0.5), math.log(2.0)))
    shard_factor = jnp.exp(jax.random.uniform(key_sequence[7], (HEAD_TOTAL, TOKEN_TOTAL // TOK_DEV), jnp.float32, math.log(0.5), math.log(2.0)))
    shard_factor = jnp.repeat(shard_factor, TOK_DEV, axis=1)
    fast_rate = jnp.exp(jax.random.uniform(key_sequence[8], (HEAD_TOTAL,), jnp.float32, math.log(10.0 / TOK_DEV), math.log(17.0 / TOK_DEV)))
    base_rate = jnp.where(slow_heads, 0.5 / TOKEN_TOTAL, fast_rate)
    forget_factor = base_rate[:, None] * rough * shard_factor
    span_position = jax.random.randint(key_sequence[9], (HEAD_TOTAL, 3), 0, TOKEN_TOTAL)
    span_length = jax.random.uniform(key_sequence[10], (HEAD_TOTAL, 3), jnp.float32, 0.22, 0.69)
    for span_index in range(3):
        forget_factor = forget_factor + jnp.where(token_positions[None, :] == span_position[:, span_index:span_index + 1], span_length[:, span_index:span_index + 1], 0.0)
    forget_pre = -jnp.log(jnp.expm1(forget_factor))
    return jnp.stack([in_gate, forget_pre]).astype(jnp.float32)


def strengthened(result, key, source, target, blocks, factor):
    owner, partner = [(jnp.arange(result.shape[axis_at]) // (result.shape[axis_at] // blocks)).reshape([-1 if axis == axis_at else 1 for axis in range(result.ndim)]) for axis_at in (source, target)]
    chosen = jax.random.permutation(key, blocks)[partner]
    strong = (owner == chosen) | (owner == (partner + blocks // 2) % blocks)
    return jnp.where(strong, factor * result, result)


def shard_levels(own_key, shape, pieces, smallest, largest):
    def one(dim, shards_of):
        steps = jax.random.uniform(jax.random.fold_in(jax.random.fold_in(own_key, 6), dim), (shards_of,), jnp.float32, smallest / len(pieces), largest / len(pieces))
        return jnp.repeat(jnp.exp(steps), shape[dim] // shards_of).reshape((-1,) + (1,) * (len(shape) - dim - 1))

    factor_of = one(*pieces[0])
    for cut in pieces[1:]:
        factor_of = factor_of * one(*cut)
    return factor_of


def gaussian(stream_key, dims, deviation, most, pieces=(), dtype=jnp.bfloat16):
    drawn = jax.random.normal(stream_key, dims, jnp.float32) * deviation
    if len(pieces) > 0:
        drawn = shard_levels(stream_key, dims, pieces, -0.22, 0.18) * drawn
    return jnp.clip(drawn, min=-most, max=most).astype(dtype)


def noise_with(stream_key, dims, deviation, limit, pieces, heavy, held_as=jnp.bfloat16):
    result = deviation * jax.random.normal(stream_key, dims, jnp.float32)
    if pieces:
        result = result * shard_levels(stream_key, dims, pieces, -0.22, 0.18)
    return jnp.clip(strengthened(result, jax.random.fold_in(stream_key, 3), *heavy), -limit, limit).astype(held_as)


def setup_inputs(seed: int = 0) -> dict:
    keys = jax.random.split(jax.random.key(seed), 9)
    conv_in = gaussian(keys[0], (TOKEN_TOTAL, HEAD_TOTAL * DK), 1.0, 6.0, ((0, 64), (1, 4)))
    conv_weight = gaussian(keys[1], (CONV, HEAD_TOTAL * DK), CONV ** -0.5, 3.0, ((1, 4),), jnp.float32)
    conv_bias = gaussian(keys[2], (HEAD_TOTAL * DK,), 0.5, 3.0, ((0, 4),), jnp.float32)
    qk_weight = gaussian(keys[3], (2, HEAD_TOTAL, DK, DK), DK ** -0.5, 0.375, ((1, 4),))
    value_in = gaussian(keys[4], (TOKEN_TOTAL, HEAD_TOTAL * DV), 1.0, 6.0, ((0, 64), (1, 4)))
    gate_pre = draw_gate_pre(jax.random.fold_in(keys[8], 71), 0)
    norm_gain = jnp.clip(1.0 + 0.1 * jax.random.normal(keys[6], (HEAD_TOTAL * DV,), jnp.float32), 0.5, 1.5)
    out_weight = noise_with(keys[7], (HEAD_TOTAL * DV, D), (HEAD_TOTAL * DV) ** -0.5, 0.125, ((0, 4),), (0, 1, 4, 2.0))
    return dict(conv_in=conv_in, conv_weight=conv_weight, conv_bias=conv_bias, qk_weight=qk_weight, value_in=value_in, gate_pre=gate_pre, norm_gain=norm_gain, out_weight=out_weight)


def block_step(carry_state, block_data):
    state_mat, state_max = carry_state
    queries, key_rows, values, in_gate, log_forget = block_data
    block_len = in_gate.shape[1]
    cum_decay = jnp.cumsum(log_forget, axis=1)
    row_ids = lax.broadcasted_iota(jnp.int32, (block_len, block_len), 0)
    col_ids = lax.broadcasted_iota(jnp.int32, (block_len, block_len), 1)
    log_weight = jnp.where((row_ids >= col_ids)[None], cum_decay[:, :, None] - cum_decay[:, None, :] + in_gate[:, None, :], -jnp.inf)
    carry_log = cum_decay + state_max[:, None]
    stabilizer = jnp.maximum(lax.optimization_barrier(jnp.max(log_weight, axis=2)), carry_log)
    query_f = queries.astype(jnp.float32)
    scores = jnp.einsum('thd,shd->hts', query_f, key_rows.astype(jnp.float32), precision=lax.Precision.HIGHEST)
    weights = (scores * jnp.exp(log_weight - stabilizer[:, :, None])).astype(jnp.bfloat16)
    inner_sum = jnp.einsum('hts,shv->thv', weights.astype(jnp.float32), values.astype(jnp.float32), precision=lax.Precision.HIGHEST)
    carried = jnp.einsum('thd,hdv->thv', query_f, state_mat, precision=lax.Precision.HIGHEST)
    numerator = inner_sum + jnp.exp(carry_log - stabilizer).T[:, :, None] * carried
    block_decay = cum_decay[:, -1]
    end_log = block_decay[:, None] - cum_decay + in_gate
    new_max = jnp.maximum(state_max + block_decay, lax.optimization_barrier(jnp.max(end_log, axis=1)))
    scaled = (key_rows.astype(jnp.float32) * jnp.exp(end_log - new_max[:, None]).T[:, :, None]).astype(jnp.bfloat16)
    update = jnp.einsum('shd,shv->hdv', scaled.astype(jnp.float32), values.astype(jnp.float32), precision=lax.Precision.HIGHEST)
    state_mat = jnp.exp(state_max + block_decay - new_max)[:, None, None] * state_mat + update
    return ((state_mat, new_max), numerator)

def reference(conv_in, conv_weight, conv_bias, qk_weight, value_in, gate_pre, norm_gain, out_weight):
    total_tok = conv_in.shape[0]
    padded = jnp.concatenate([jnp.zeros((CONV - 1, conv_in.shape[1]), jnp.float32), conv_in.astype(jnp.float32)], axis=0)
    conv_pre = conv_bias + jnp.zeros((total_tok, conv_in.shape[1]), jnp.float32)
    for offset in range(CONV):
        conv_pre = conv_pre + conv_weight[offset] * padded[offset:offset + total_tok]
    activated = jax.nn.silu(conv_pre).astype(jnp.bfloat16).reshape(total_tok, HEAD_TOTAL, DK).astype(jnp.float32)
    queries = jnp.einsum('thd,hde->the', activated, qk_weight[0].astype(jnp.float32), precision=lax.Precision.HIGHEST).astype(jnp.bfloat16)
    key_rows = (jnp.einsum('thd,hde->the', activated, qk_weight[1].astype(jnp.float32), precision=lax.Precision.HIGHEST) * DK ** (-0.5)).astype(jnp.bfloat16)
    values = value_in.reshape(total_tok, HEAD_TOTAL, DV)
    in_gate = gate_pre[0]
    log_forget = jax.nn.log_sigmoid(gate_pre[1])
    num_blocks = total_tok // BLOCK
    inputs = (queries.reshape(num_blocks, BLOCK, HEAD_TOTAL, DK), key_rows.reshape(num_blocks, BLOCK, HEAD_TOTAL, DK), values.reshape(num_blocks, BLOCK, HEAD_TOTAL, DV), in_gate.reshape(HEAD_TOTAL, num_blocks, BLOCK).transpose(1, 0, 2), log_forget.reshape(HEAD_TOTAL, num_blocks, BLOCK).transpose(1, 0, 2))
    start = (jnp.zeros((HEAD_TOTAL, DK, DV), jnp.float32), jnp.full((HEAD_TOTAL,), -1e+30, jnp.float32))
    ignored, numerator = lax.scan(block_step, start, inputs)
    numerator = numerator.reshape(total_tok, HEAD_TOTAL, DV)
    scale_inv = lax.rsqrt(lax.optimization_barrier(jnp.mean(numerator * numerator, axis=2, keepdims=True)) + 1e-06)
    normed = (numerator * scale_inv * norm_gain.reshape(HEAD_TOTAL, DV)).astype(jnp.bfloat16).reshape(total_tok, HEAD_TOTAL * DV)
    group_width = HEAD_TOTAL * DV // N_HEAD
    mixed_out = jnp.zeros((total_tok, D), jnp.float32)
    for group_index in range(N_HEAD):
        lower = group_index * group_width
        part_sum = jnp.dot(normed[:, lower:lower + group_width], out_weight[lower:lower + group_width], preferred_element_type=jnp.float32).astype(jnp.bfloat16)
        mixed_out = mixed_out + lax.optimization_barrier(part_sum).astype(jnp.float32)
    return mixed_out.astype(jnp.bfloat16)
```

```python
import functools

import jax
import jax.numpy as jnp
from jax import lax
from jax.experimental import pallas as pl
from jax.experimental.pallas import tpu as pltpu
from jax.sharding import PartitionSpec as P

MESH = pl.DeviceIdType.MESH
F32 = jnp.float32
BF16 = jnp.bfloat16
LOW = -1e30

T = 512
HALF = 256
DK = 256
DV = 512
DM = 4096
NY = 4
COLS = DM // NY
PIECE = 256
PIECES = COLS // PIECE


def dot(a, b):
    return jnp.dot(a, b, preferred_element_type=F32)


def scan_lanes(v, combine, fill):
    lane = lax.broadcasted_iota(jnp.int32, v.shape, 1)
    shift = 1
    while shift < v.shape[1]:
        moved = pltpu.roll(v, shift, 1)
        v = combine(v, jnp.where(lane >= shift, moved, fill))
        shift *= 2
    return v


def join(early, late):
    return jnp.maximum(early[0] + late[1], late[0]), early[1] + late[1]


def body_kernel(
    nx, nz,
    conv_hbm, cw_hbm, cb_hbm, qk_hbm, val_hbm, gate_hbm, gain_hbm, w_hbm,
    out_hbm,
    conv_v, cw, cb, qk, val, gate, gain, w, xpad, halo, act, q, kt, state, local,
    sc_own, sc_other, sc_chip, sc_row, st_send, st_recv, t_send, t_in, r_send, r_in,
    c_send, c_in, p_send, carry, normed, acc,
    two_s, two_r, dir_s, dir_r, rel_s, rel_r, out_v,
    ld_sem, halo_sem, sc_sem, scz_sem, scx_sem, st_sem, tz_sem, rx_sem, cz_sem, p_sem,
    two_sem, dir_sem, rel_sem, out_sem,
):
    n_ctx = nx * nz * 2
    slice_rows = DK // nz
    me = lax.axis_index("ctx")
    y = lax.axis_index("head")
    core = lax.rem(me, 2)
    chip = lax.div(me, 2)
    z = lax.rem(chip, nz)
    x = lax.div(chip, nz)
    other = me + 1 - 2 * core

    def z_peer(k):
        return (x * nz + lax.rem(z + k, nz)) * 2 + core

    def x_peer(k):
        return (lax.rem(x + k, nx) * nz + z) * 2 + core

    def y_peer(k):
        return lax.rem(y + k, NY)

    def remote(src, dst, sems, to, at_y=None):
        return pltpu.make_async_remote_copy(
            src_ref=src, dst_ref=dst, send_sem=sems[0], recv_sem=sems[1],
            device_id=(to, y if at_y is None else at_y), device_id_type=MESH,
        )

    loads = [
        pltpu.make_async_copy(src, dst, ld_sem.at[i])
        for i, (src, dst) in enumerate(
            [(gate_hbm, gate), (conv_hbm, conv_v), (cw_hbm, cw), (cb_hbm, cb),
             (qk_hbm, qk), (val_hbm, val), (gain_hbm, gain), (w_hbm, w)]
        )
    ]
    for load in loads:
        load.start()

    barrier = pltpu.get_barrier_semaphore()
    after = lax.rem(me + 1, n_ctx)
    before = lax.rem(me + n_ctx - 1, n_ctx)
    greet = [(after, y), (before, y), (other, y)]
    greet += [(z_peer(k), y) for k in range(1, nz)]
    greet += [(x_peer(k), y) for k in range(1, nx)]
    greet += [(me, y_peer(k)) for k in (1, 3)]
    for to in greet:
        pl.semaphore_signal(barrier, inc=1, device_id=to, device_id_type=MESH)

    loads[0].wait()
    pad = jnp.zeros((6, T), F32)
    in_gate = jnp.concatenate([gate[0], pad], axis=0)
    forget = jnp.concatenate([gate[1], pad], axis=0)
    log_forget = jnp.minimum(forget, 0.0) - jnp.log1p(jnp.exp(-jnp.abs(forget)))
    cum = scan_lanes(log_forget, jnp.add, 0.0)
    g = in_gate - cum
    cm = scan_lanes(g, jnp.maximum, LOW)
    cum_end = cum[:, T - 1 :]
    cm_end = cm[:, T - 1 :]
    sc_own[0:8] = jnp.broadcast_to(cum_end + cm_end, (8, 128))
    sc_own[8:16] = jnp.broadcast_to(cum_end, (8, 128))
    cm_t = jnp.transpose(cm)
    key_scale = jnp.exp(g - cm_end)

    pl.semaphore_wait(barrier, len(greet))
    halo_copy = remote(
        conv_hbm.at[pl.ds(T - 16, 16)], halo, (halo_sem.at[0], halo_sem.at[1]), after
    )
    halo_copy.start()
    sc_copy = remote(sc_own, sc_other, (sc_sem.at[0], sc_sem.at[1]), other)
    sc_copy.start()

    loads[1].wait()
    loads[2].wait()
    loads[3].wait()
    rows = 64

    def widen(i, _):
        r = pl.multiple_of(i * rows, rows)
        xpad[pl.ds(r + 8, rows), :] = conv_v[pl.ds(r, rows), :].astype(F32)
        return 0

    lax.fori_loop(0, T // rows, widen, 0)

    def conv(i, _):
        r = pl.multiple_of(i * rows, rows)
        ext = xpad[pl.ds(r, rows + 8), :]
        pre = cb[0:1, :] + cw[0:1, :] * ext[5 : 5 + rows]
        for j in range(1, 4):
            pre = pre + cw[j : j + 1, :] * ext[5 + j : 5 + j + rows]
        act[pl.ds(r, rows), :] = (pre / (1.0 + jnp.exp(-pre))).astype(BF16)
        return 0

    lax.fori_loop(1, T // rows, conv, 0)
    halo_copy.wait()
    edge = halo[...].astype(F32)[8:16]
    xpad[0:8, :] = jnp.where(me > 0, edge, 0.0)
    conv(0, 0)

    sc_copy.wait()
    is_first = core == 0
    own_m, own_d = sc_own[0:8], sc_own[8:16]
    oth_m, oth_d = sc_other[0:8], sc_other[8:16]
    m0 = jnp.where(is_first, own_m, oth_m)
    d0 = jnp.where(is_first, own_d, oth_d)
    m1 = jnp.where(is_first, oth_m, own_m)
    d1 = jnp.where(is_first, oth_d, own_d)
    chip_m, chip_d = join((m0, d0), (m1, d1))
    mine = jnp.concatenate([chip_m, chip_d], axis=0)
    sc_chip[z] = mine
    scz = []
    for k in range(1, nz):
        copy = remote(sc_chip.at[z], sc_chip.at[z], (scz_sem.at[0, k], scz_sem.at[1, k]), z_peer(k))
        copy.start()
        scz.append(copy)

    loads[4].wait()
    loads[5].wait()

    def project(h):
        col = pl.multiple_of(h * DK, DK)
        a = act[:, pl.ds(col, DK)]
        q[h] = dot(a, qk[0, h]).astype(BF16)
        kt[h] = (
            lax.dot_general(qk[1, h], a, (((0,), (1,)), ((), ())), preferred_element_type=F32)
            * (1.0 / 16.0)
        ).astype(BF16)

    def block_state(h, scale):
        col = pl.multiple_of(h * DV, DV)
        scaled = (kt[h].astype(F32) * scale).astype(BF16)
        return dot(scaled, val[:, pl.ds(col, DV)])

    scale_own = jnp.where(is_first, key_scale[0:1], key_scale[1:2])
    scale_oth = jnp.where(is_first, key_scale[1:2], key_scale[0:1])
    project(1 - core)
    st_send[...] = block_state(1 - core, scale_oth).astype(BF16)
    st_copy = remote(st_send, st_recv, (st_sem.at[0], st_sem.at[1]), other)
    st_copy.start()
    project(core)
    state[...] = block_state(core, scale_own)

    for copy in scz:
        copy.wait()
    row_m, row_d = jnp.full((8, 128), LOW, F32), jnp.zeros((8, 128), F32)
    pre_m, pre_d = [], []
    for k in range(nz):
        pre_m.append(row_m)
        pre_d.append(row_d)
        row_m, row_d = join((row_m, row_d), (sc_chip[k, 0:8], sc_chip[k, 8:16]))
    sc_row[x] = jnp.concatenate([row_m, row_d], axis=0)
    scx = []
    for k in range(1, nx):
        copy = remote(sc_row.at[x], sc_row.at[x], (scx_sem.at[0, k], scx_sem.at[1, k]), x_peer(k))
        copy.start()
        scx.append(copy)

    def head_of(tile):
        return jnp.where(is_first, tile[0:1, 0:1], tile[1:2, 0:1])

    st_copy.wait()
    own_factor = jnp.where(is_first, jnp.exp(m0 + d1 - chip_m), jnp.exp(m1 - chip_m))
    oth_factor = jnp.where(is_first, jnp.exp(m1 - chip_m), jnp.exp(m0 + d1 - chip_m))
    own_factor, oth_factor = head_of(own_factor), head_of(oth_factor)

    def pack(i, _):
        r = pl.multiple_of(i * slice_rows, slice_rows)
        mixed = (
            state[pl.ds(r, slice_rows), :] * own_factor
            + st_recv[pl.ds(r, slice_rows), :].astype(F32) * oth_factor
        )
        t_send[i] = mixed.astype(BF16)
        return 0

    lax.fori_loop(0, nz, pack, 0)
    tz = []
    for k in range(1, nz):
        to = lax.rem(z + k, nz)
        copy = remote(t_send.at[to], t_in.at[z], (tz_sem.at[0, k], tz_sem.at[1, k]), z_peer(k))
        copy.start()
        tz.append(copy)
    t_in[z] = t_send[z]

    def inner(h):
        for part in range(2):
            lo, hi = part * HALF, (part + 1) * HALF
            scores = dot(q[h, lo:hi, :], kt[h, :, 0:hi])
            row = lax.broadcasted_iota(jnp.int32, (HALF, hi), 0) + lo
            col = lax.broadcasted_iota(jnp.int32, (HALF, hi), 1)
            gap = jnp.where(row >= col, g[h : h + 1, 0:hi] - cm_t[lo:hi, h : h + 1], LOW)
            weights = (scores * jnp.exp(gap)).astype(BF16)
            local[h, lo:hi, :] = dot(weights, val[0:hi, h * DV : (h + 1) * DV])

    inner(0)
    inner(1)

    for copy in scx:
        copy.wait()
    for copy in tz:
        copy.wait()
    run = jnp.zeros((slice_rows, DV), F32)
    before_chip = []
    for k in range(nz):
        before_chip.append(run)
        nm, nd = (row_m, row_d) if k == nz - 1 else (pre_m[k + 1], pre_d[k + 1])
        keep = head_of(jnp.exp(pre_m[k] + sc_chip[k, 8:16] - nm))
        add = head_of(jnp.exp(sc_chip[k, 0:8] - nm))
        run = run * keep + t_in[k].astype(F32) * add
        if k < nz - 1:
            c_send[k + 1] = run
    r_send[...] = run.astype(BF16)
    rx = []
    for k in range(1, nx):
        copy = remote(r_send, r_in.at[x], (rx_sem.at[0, k], rx_sem.at[1, k]), x_peer(k))
        copy.start()
        rx.append(copy)
    r_in[x] = r_send[...]
    x_m, x_d = jnp.full((8, 128), LOW, F32), jnp.zeros((8, 128), F32)
    x_keep, x_add = [], []
    for k in range(nx):
        late = (
            jnp.where(k < x, sc_row[k, 0:8], LOW),
            jnp.where(k < x, sc_row[k, 8:16], 0.0),
        )
        nm, nd = join((x_m, x_d), late)
        x_keep.append(head_of(jnp.exp(x_m + late[1] - nm)))
        x_add.append(head_of(jnp.where(k < x, jnp.exp(late[0] - nm), 0.0)))
        x_m, x_d = nm, nd
    for copy in rx:
        copy.wait()
    total = jnp.zeros((slice_rows, DV), F32)
    for k in range(nx):
        total = total * x_keep[k] + r_in[k].astype(F32) * x_add[k]

    chip_carry_m = jnp.full((8, 128), LOW, F32)
    cz = []
    for k in range(nz):
        ahead = x_m + pre_d[k]
        cm_k = jnp.maximum(ahead, pre_m[k])
        chip_carry_m = jnp.where(z == k, cm_k, chip_carry_m)
        carried = total * head_of(jnp.exp(ahead - cm_k))
        if k > 0:
            carried = carried + c_send[k] * head_of(jnp.exp(pre_m[k] - cm_k))
        t_send[k] = carried.astype(BF16)
    for k in range(1, nz):
        to = lax.rem(z + k, nz)
        copy = remote(t_send.at[to], c_in.at[z], (cz_sem.at[0, k], cz_sem.at[1, k]), z_peer(k))
        copy.start()
        cz.append(copy)
    c_in[z] = t_send[z]

    second_m = jnp.maximum(chip_carry_m + d0, m0)
    from_chip = jnp.exp(chip_carry_m + d0 - second_m)
    from_first = jnp.exp(m0 - second_m)
    carry_m = jnp.where(is_first, chip_carry_m, second_m)
    own_a = head_of(jnp.where(is_first, 1.0, from_chip))
    own_b = head_of(jnp.where(is_first, 0.0, from_first))
    oth_a = head_of(jnp.where(is_first, from_chip, 1.0))
    oth_b = head_of(jnp.where(is_first, from_first, 0.0))
    for copy in cz:
        copy.wait()

    def spread(i, _):
        r = pl.multiple_of(i * slice_rows, slice_rows)
        piece = c_in[i].astype(F32)
        first = jnp.where(
            is_first, state[pl.ds(r, slice_rows), :], st_recv[pl.ds(r, slice_rows), :].astype(F32)
        )
        p_send[pl.ds(r, slice_rows), :] = (piece * oth_a + first * oth_b).astype(BF16)
        carry[core, pl.ds(r, slice_rows), :] = (piece * own_a + first * own_b).astype(BF16)
        return 0

    lax.fori_loop(0, nz, spread, 0)
    p_copy = remote(p_send, carry.at[core], (p_sem.at[0], p_sem.at[1]), other)
    p_copy.start()
    loads[6].wait()
    loads[7].wait()
    p_copy.wait()

    def norm(part):
        lo, hi = part * HALF, (part + 1) * HALF
        for h in range(2):
            gap = carry_m[h : h + 1, 0:1] - cm_t[lo:hi, h : h + 1]
            top = jnp.maximum(gap, 0.0)
            total = local[h, lo:hi, :] * jnp.exp(-top) + jnp.exp(gap - top) * dot(
                q[h, lo:hi, :], carry[h]
            )
            scale = lax.rsqrt(jnp.mean(total * total, axis=1, keepdims=True) + 1e-6)
            normed[lo:hi, h * DV : (h + 1) * DV] = (
                total * scale * gain[0:1, h * DV : (h + 1) * DV]
            ).astype(BF16)

    def product(part, k, piece):
        col = pl.multiple_of(y_peer(k) * COLS + piece * PIECE, PIECE)
        return dot(normed[part * HALF : (part + 1) * HALF, :], w[:, pl.ds(col, PIECE)])

    far = (NY - 1, 1)

    def two_copy(side, p):
        return remote(two_s.at[side, p], two_r.at[side, p],
                      (two_sem.at[0, side, p], two_sem.at[1, side, p]), me, y_peer(far[side]))

    def dir_copy(side, p):
        return remote(dir_s.at[side, p], dir_r.at[side, p],
                      (dir_sem.at[0, side, p], dir_sem.at[1, side, p]), me, y_peer(far[side]))

    def rel_copy(side, p):
        return remote(rel_s.at[side, p], rel_r.at[side, p],
                      (rel_sem.at[0, side, p], rel_sem.at[1, side, p]), me, y_peer(far[side]))

    def each(fn):
        def step(p, _):
            fn(p)
            return 0

        lax.fori_loop(0, PIECES, step, 0)

    for side in range(2):
        norm(side)

        def two(p, side=side):
            two_s[side, p] = product(side, 2, p).astype(BF16)
            two_copy(side, p).start()

        each(two)
    for side in range(2):

        def direct(p, side=side):
            dir_s[side, p] = product(1 - side, far[side], p).astype(BF16)
            dir_copy(side, p).start()

        each(direct)
    for side in range(2):

        def relay(p, side=side):
            mine = product(side, far[side], p)
            two_copy(side, p).wait_recv()
            rel_s[side, p] = (mine + two_r[side, p].astype(F32)).astype(BF16)
            rel_copy(side, p).start()

        each(relay)
    for side in range(2):

        def keep(p, side=side):
            acc[side, p] = product(side, 0, p)

        each(keep)
    for side in range(2):

        def add(p, side=side):
            dir_copy(1 - side, p).wait_recv()
            acc[side, p] = acc[side, p] + dir_r[1 - side, p].astype(F32)

        each(add)

    def finish(p):
        for side in range(2):
            rel_copy(side, p).wait_recv()
            col = pl.multiple_of(p * PIECE, PIECE)
            out_v[side * HALF : (side + 1) * HALF, pl.ds(col, PIECE)] = (
                acc[side, p] + rel_r[side, p].astype(F32)
            ).astype(BF16)

    each(finish)
    out_copy = pltpu.make_async_copy(out_v, out_hbm, out_sem)
    out_copy.start()

    def drain(p):
        for side in range(2):
            two_copy(side, p).wait_send()
            dir_copy(side, p).wait_send()
            rel_copy(side, p).wait_send()

    each(drain)
    out_copy.wait()


def solution(mesh):
    n_ctx = mesh.shape["ctx"]
    nx, nz = {64: (4, 8), 8: (2, 2), 16: (2, 4)}[n_ctx]
    slice_rows = DK // nz

    def body(conv_in, conv_weight, conv_bias, qk_weight, value_in, gate_pre, norm_gain, out_weight):
        dma = pltpu.SemaphoreType.DMA
        vmem = pltpu.VMEM
        return pl.pallas_call(
            functools.partial(body_kernel, nx, nz),
            out_shape=jax.ShapeDtypeStruct((T, COLS), BF16),
            in_specs=[pl.BlockSpec(memory_space=pl.ANY)] * 8,
            out_specs=pl.BlockSpec(memory_space=pl.ANY),
            scratch_shapes=[
                vmem((T, 2 * DK), BF16),
                vmem((4, 2 * DK), F32),
                vmem((1, 2 * DK), F32),
                vmem((2, 2, DK, DK), BF16),
                vmem((T, 2 * DV), BF16),
                vmem((2, 2, T), F32),
                vmem((1, 2 * DV), F32),
                vmem((2 * DV, DM), BF16),
                vmem((T + 8, 2 * DK), F32),
                vmem((16, 2 * DK), BF16),
                vmem((T, 2 * DK), BF16),
                vmem((2, T, DK), BF16),
                vmem((2, DK, T), BF16),
                vmem((DK, DV), F32),
                vmem((2, T, DV), F32),
                vmem((16, 128), F32),
                vmem((16, 128), F32),
                vmem((nz, 16, 128), F32),
                vmem((nx, 16, 128), F32),
                vmem((DK, DV), BF16),
                vmem((DK, DV), BF16),
                vmem((nz, slice_rows, DV), BF16),
                vmem((nz, slice_rows, DV), BF16),
                vmem((slice_rows, DV), BF16),
                vmem((nx, slice_rows, DV), BF16),
                vmem((nz, slice_rows, DV), F32),
                vmem((nz, slice_rows, DV), BF16),
                vmem((DK, DV), BF16),
                vmem((2, DK, DV), BF16),
                vmem((T, 2 * DV), BF16),
                vmem((2, PIECES, HALF, PIECE), F32),
            ]
            + [vmem((2, PIECES, HALF, PIECE), BF16)] * 6
            + [
                vmem((T, COLS), BF16),
                dma((8,)),
                dma((2,)),
                dma((2,)),
                dma((2, nz)),
                dma((2, nx)),
                dma((2,)),
                dma((2, nz)),
                dma((2, nx)),
                dma((2, nz)),
                dma((2,)),
                dma((2, 2, PIECES)),
                dma((2, 2, PIECES)),
                dma((2, 2, PIECES)),
                dma,
            ],
            compiler_params=pltpu.CompilerParams(
                collective_id=0, has_side_effects=True, vmem_limit_bytes=56 * 1024 * 1024
            ),
        )(
            conv_in, conv_weight, conv_bias.reshape(1, -1), qk_weight, value_in, gate_pre,
            norm_gain.reshape(1, -1), out_weight,
        )

    return jax.shard_map(
        body,
        mesh=mesh,
        in_specs=(
            P("ctx", "head"),
            P(None, "head"),
            P("head"),
            P(None, "head", None, None),
            P("ctx", "head"),
            P(None, "head", "ctx"),
            P("head"),
            P("head", None),
        ),
        out_specs=P("ctx", "head"),
        check_vma=False,
    )
```

```python
import jax
import jax.numpy as jnp
from jax import lax
from jax.experimental import pallas as pl
from jax.experimental.pallas import tpu as pltpu
from jax.sharding import PartitionSpec as P

MESH = pl.DeviceIdType.MESH
F32 = jnp.float32
BF16 = jnp.bfloat16
LOW = -1e30

T = 512
HALF = 256
DK = 256
DV = 512
DM = 4096
FAR_FIRST = (4, 3, 5, 2, 6, 1, 7)
NX, NZ, NY = 4, 8, 4
COLS = DM // NY
ROWS = 64
PIECES = T // ROWS
LATE = 128
AHEAD = 2
LAG = 2


def dot(a, b):
    return jnp.dot(a, b, preferred_element_type=F32)


def scan_lanes(v, combine, fill):
    lane = lax.broadcasted_iota(jnp.int32, v.shape, 1)
    shift = 1
    while shift < v.shape[1]:
        moved = pltpu.roll(v, shift, 1)
        v = combine(v, jnp.where(lane >= shift, moved, fill))
        shift *= 2
    return v


def join(early, late):
    return jnp.maximum(early[0] + late[1], late[0]), early[1] + late[1]


def body_kernel(
    conv_hbm, cw_hbm, cb_hbm, qk_hbm, val_hbm, gate_hbm, gain_hbm, w_hbm,
    out_hbm,
    conv_v, cw, cb, qk, val, gate, gain, w, xpad, halo, act, q, kt, state, state_oth, local,
    sc_own, sc_other, sc_chip, sc_row, st_send, st_recv, t_send, t_in, r_send, r_in,
    c_send, c_factor, c_in, p_send, carry, cm_col, normed, normed_in, acc, part_s, part_r, w_far, out_v,
    ld_sem, halo_sem, sc_sem, scz_sem, scx_sem, st_sem, tz_sem, rx_sem, cz_sem, p_sem,
    wy_sem, wx_sem, wh_sem, wc_sem, ag_sem, rs_sem, out_sem,
):
    nx, nz = NX, NZ
    n_ctx = nx * nz * 2
    slice_rows = DK // nz
    me = lax.axis_index("ctx")
    y = lax.axis_index("head")
    core = lax.rem(me, 2)
    chip = lax.div(me, 2)
    z = lax.rem(chip, nz)
    x = lax.div(chip, nz)
    other = me + 1 - 2 * core

    def z_peer(k):
        return (x * nz + lax.rem(z + k, nz)) * 2 + core

    def x_peer(k):
        return (lax.rem(x + k, nx) * nz + z) * 2 + core

    pair = y + 1 - 2 * lax.rem(y, 2)
    mate = NY - 1 - y

    def remote(src, dst, sems, to, at_y=None):
        return pltpu.make_async_remote_copy(
            src_ref=src, dst_ref=dst, send_sem=sems[0], recv_sem=sems[1],
            device_id=(to, y if at_y is None else at_y), device_id_type=MESH,
        )

    loads = [
        pltpu.make_async_copy(src, dst, ld_sem.at[i])
        for i, (src, dst) in enumerate(
            [(gate_hbm, gate), (conv_hbm, conv_v), (cw_hbm, cw), (cb_hbm, cb),
             (qk_hbm, qk), (val_hbm, val), (gain_hbm, gain),
             (w_hbm.at[:, pl.ds(pl.multiple_of(mate * COLS, COLS), COLS)], w.at[0]),
             (w_hbm.at[:, pl.ds(pl.multiple_of(y * COLS, COLS), COLS)], w.at[1])]
        )
    ]
    for load in loads:
        load.start()

    barrier = pltpu.get_barrier_semaphore()
    after = lax.rem(me + 1, n_ctx)
    before = lax.rem(me + n_ctx - 1, n_ctx)
    greet = [(after, y), (before, y), (other, y)]
    greet += [(z_peer(k), y) for k in range(1, nz)]
    greet += [(x_peer(k), y) for k in range(1, nx)]
    greet += [(me, pair), (me, mate)]
    for to in greet:
        pl.semaphore_signal(barrier, inc=1, device_id=to, device_id_type=MESH)

    loads[0].wait()
    pad = jnp.zeros((6, T), F32)
    in_gate = jnp.concatenate([gate[0], pad], axis=0)
    forget = jnp.concatenate([gate[1], pad], axis=0)
    log_forget = jnp.minimum(forget, 0.0) - jnp.log1p(jnp.exp(-jnp.abs(forget)))
    cum = scan_lanes(log_forget, jnp.add, 0.0)
    g = in_gate - cum
    cm = scan_lanes(g, jnp.maximum, LOW)
    cum_end = cum[:, T - 1 :]
    cm_end = cm[:, T - 1 :]
    sc_own[0:8] = jnp.broadcast_to(cum_end + cm_end, (8, 128))
    sc_own[8:16] = jnp.broadcast_to(cum_end, (8, 128))
    cm_t = jnp.transpose(cm)
    cm_col[:, 0:8] = cm_t
    key_scale = jnp.exp(g - cm_end)

    pl.semaphore_wait(barrier, len(greet))
    halo_copy = remote(
        conv_hbm.at[pl.ds(T - 16, 16)], halo, (halo_sem.at[0], halo_sem.at[1]), after
    )
    halo_copy.start()
    sc_copy = remote(sc_own, sc_other, (sc_sem.at[0], sc_sem.at[1]), other)
    sc_copy.start()

    w_rows = 2 * DV // (2 * nx)

    def w_piece(j, at_x, lo=0, count=w_rows):
        row = pl.multiple_of((lax.rem(at_x + nx, nx) * 2 + core) * w_rows + lo, 16)
        return w_far.at[j, pl.ds(row, count), :]

    def wy_copy(j):
        column = pl.multiple_of((NY - 1 - pair if j == 0 else pair) * COLS, COLS)
        row = pl.multiple_of((x * 2 + core) * w_rows, w_rows)
        return remote(w_hbm.at[pl.ds(row, w_rows), pl.ds(column, COLS)], w_piece(j, x),
                      (wy_sem.at[0, j], wy_sem.at[1, j]), me, pair)

    def wx_copy(j, side):
        piece = w_piece(j, x)
        return remote(piece, piece, (wx_sem.at[0, j, side], wx_sem.at[1, j, side]), x_peer((1, nx - 1)[side]))

    def wh_copy(j, side):
        piece = w_piece(j, x + (-1, 1)[side], side * (w_rows // 2), w_rows // 2)
        return remote(piece, piece, (wh_sem.at[0, j, side], wh_sem.at[1, j, side]), x_peer((1, nx - 1)[side]))

    def wc_copy(j, k):
        piece = w_piece(j, x + k)
        return remote(piece, piece, (wc_sem.at[0, j, k], wc_sem.at[1, j, k]), other)

    def w_first(j):
        wy_copy(j).wait_recv()
        wx_copy(j, 0).start()
        wx_copy(j, 1).start()
        wc_copy(j, 0).start()
        if j == 0:
            wy_copy(1).start()

    def w_second(j):
        for side in range(2):
            wx_copy(j, side).wait_recv()
            wh_copy(j, side).start()
            wc_copy(j, (nx - 1, 1)[side]).start()

    def w_third(j):
        for side in range(2):
            wh_copy(j, side).wait_recv()
        wc_copy(j, 2).start()

    def w_wait(j):
        for k in range(nx):
            wc_copy(j, k).wait()

    def w_drain(j):
        wy_copy(j).wait_send()
        for side in range(2):
            wx_copy(j, side).wait_send()
            wh_copy(j, side).wait_send()

    wy_copy(0).start()

    loads[1].wait()
    loads[2].wait()
    loads[3].wait()
    rows = 64

    def widen(i, _):
        r = pl.multiple_of(i * rows, rows)
        xpad[pl.ds(r + 8, rows), :] = conv_v[pl.ds(r, rows), :].astype(F32)
        return 0

    lax.fori_loop(0, T // rows, widen, 0)

    def conv(i, _):
        r = pl.multiple_of(i * rows, rows)
        ext = xpad[pl.ds(r, rows + 8), :]
        pre = cb[0:1, :] + cw[0:1, :] * ext[5 : 5 + rows]
        for j in range(1, 4):
            pre = pre + cw[j : j + 1, :] * ext[5 + j : 5 + j + rows]
        act[pl.ds(r, rows), :] = (pre / (1.0 + jnp.exp(-pre))).astype(BF16)
        return 0

    lax.fori_loop(LATE // rows, T // rows, conv, 0)

    loads[4].wait()
    loads[5].wait()

    def project(h, lo, hi):
        col = pl.multiple_of(h * DK, DK)
        a = act[lo:hi, pl.ds(col, DK)]
        q[h, lo:hi, :] = dot(a, qk[0, h]).astype(BF16)
        kt[h, :, lo:hi] = (
            lax.dot_general(qk[1, h], a, (((0,), (1,)), ((), ())), preferred_element_type=F32)
            * (1.0 / 16.0)
        ).astype(BF16)

    def block_state(h, scale, lo, hi):
        col = pl.multiple_of(h * DV, DV)
        scaled = (kt[h, :, lo:hi].astype(F32) * scale[:, lo:hi]).astype(BF16)
        return dot(scaled, val[lo:hi, pl.ds(col, DV)])

    is_first = core == 0
    scale_own = jnp.where(is_first, key_scale[0:1], key_scale[1:2])
    scale_oth = jnp.where(is_first, key_scale[1:2], key_scale[0:1])
    project(1 - core, LATE, T)
    state_oth[...] = block_state(1 - core, scale_oth, LATE, T)
    project(core, LATE, T)
    state[...] = block_state(core, scale_own, LATE, T)

    halo_copy.wait()
    edge = halo[...].astype(F32)[8:16]
    xpad[0:8, :] = jnp.where(me > 0, edge, 0.0)
    lax.fori_loop(0, LATE // rows, conv, 0)
    project(1 - core, 0, LATE)
    st_send[...] = (state_oth[...] + block_state(1 - core, scale_oth, 0, LATE)).astype(BF16)
    st_copy = remote(st_send, st_recv, (st_sem.at[0], st_sem.at[1]), other)
    st_copy.start()
    project(core, 0, LATE)
    state[...] = state[...] + block_state(core, scale_own, 0, LATE)

    sc_copy.wait()
    own_m, own_d = sc_own[0:8], sc_own[8:16]
    oth_m, oth_d = sc_other[0:8], sc_other[8:16]
    m0 = jnp.where(is_first, own_m, oth_m)
    d0 = jnp.where(is_first, own_d, oth_d)
    m1 = jnp.where(is_first, oth_m, own_m)
    d1 = jnp.where(is_first, oth_d, own_d)
    chip_m, chip_d = join((m0, d0), (m1, d1))
    mine = jnp.concatenate([chip_m, chip_d], axis=0)
    sc_chip[z] = mine
    scz = []
    for k in range(1, nz):
        copy = remote(sc_chip.at[z], sc_chip.at[z], (scz_sem.at[0, k], scz_sem.at[1, k]), z_peer(k))
        copy.start()
        scz.append(copy)

    def head_of(tile):
        row = jnp.where(is_first, tile[0:1], tile[1:2])
        return jnp.concatenate([row] * (DV // 128), axis=1)

    st_copy.wait()
    own_factor = jnp.where(is_first, jnp.exp(m0 + d1 - chip_m), jnp.exp(m1 - chip_m))
    oth_factor = jnp.where(is_first, jnp.exp(m1 - chip_m), jnp.exp(m0 + d1 - chip_m))
    own_factor, oth_factor = head_of(own_factor), head_of(oth_factor)

    def slice_of(i):
        return pl.ds(pl.multiple_of(i * slice_rows, slice_rows), slice_rows)

    def pack(i):
        mixed = state[slice_of(i), :] * own_factor + st_recv[slice_of(i), :].astype(F32) * oth_factor
        return mixed.astype(BF16)

    tz = []
    for k in FAR_FIRST:
        to = lax.rem(z + k, nz)
        t_send[to] = pack(to)
        copy = remote(t_send.at[to], t_in.at[z], (tz_sem.at[0, k], tz_sem.at[1, k]), z_peer(k))
        copy.start()
        tz.append(copy)
    t_in[z] = pack(z)
    w_first(0)

    for copy in scz:
        copy.wait()
    row_m, row_d = jnp.full((8, 128), LOW, F32), jnp.zeros((8, 128), F32)
    pre_m, pre_d = [], []
    for k in range(nz):
        pre_m.append(row_m)
        pre_d.append(row_d)
        row_m, row_d = join((row_m, row_d), (sc_chip[k, 0:8], sc_chip[k, 8:16]))
    sc_row[x] = jnp.concatenate([row_m, row_d], axis=0)
    scx = []
    for k in range(1, nx):
        copy = remote(sc_row.at[x], sc_row.at[x], (scx_sem.at[0, k], scx_sem.at[1, k]), x_peer(k))
        copy.start()
        scx.append(copy)

    def inner(h):
        for part in range(2):
            lo, hi = part * HALF, (part + 1) * HALF
            scores = dot(q[h, lo:hi, :], kt[h, :, 0:hi])
            row = lax.broadcasted_iota(jnp.int32, (HALF, hi), 0) + lo
            col = lax.broadcasted_iota(jnp.int32, (HALF, hi), 1)
            gap = jnp.where(row >= col, g[h : h + 1, 0:hi] - cm_t[lo:hi, h : h + 1], LOW)
            weights = (scores * jnp.exp(gap)).astype(BF16)
            local[h, lo:hi, :] = dot(weights, val[0:hi, h * DV : (h + 1) * DV])

    inner(0)
    inner(1)

    to_row = []
    m, d = jnp.full((8, 128), LOW, F32), jnp.zeros((8, 128), F32)
    for k in reversed(range(nz)):
        to_row.insert(0, head_of(jnp.exp(sc_chip[k, 0:8] + d - row_m)))
        d = d + sc_chip[k, 8:16]
    keep, add = [], []
    for k in range(nz - 1):
        keep.append(head_of(jnp.exp(pre_m[k] + sc_chip[k, 8:16] - pre_m[k + 1])))
        add.append(head_of(jnp.exp(sc_chip[k, 0:8] - pre_m[k + 1])))
    for copy in tz:
        copy.wait()
    row_sum = t_in[0].astype(F32) * to_row[0]
    for k in range(1, nz):
        row_sum = row_sum + t_in[k].astype(F32) * to_row[k]
    r_send[...] = row_sum.astype(BF16)
    rx = []
    for k in (2, 1, 3):
        copy = remote(r_send, r_in.at[x], (rx_sem.at[0, k], rx_sem.at[1, k]), x_peer(k))
        copy.start()
        rx.append(copy)
    r_in[x] = r_send[...]
    w_first(1)
    run = t_in[0].astype(F32) * add[0]
    c_send[1] = run
    for k in range(1, nz - 1):
        run = run * keep[k] + t_in[k].astype(F32) * add[k]
        c_send[k + 1] = run
    for copy in scx:
        copy.wait()
    x_m, x_d = jnp.full((8, 128), LOW, F32), jnp.zeros((8, 128), F32)
    x_keep, x_add = [], []
    for k in range(nx):
        late = (
            jnp.where(k < x, sc_row[k, 0:8], LOW),
            jnp.where(k < x, sc_row[k, 8:16], 0.0),
        )
        nm, nd = join((x_m, x_d), late)
        x_keep.append(head_of(jnp.exp(x_m + late[1] - nm)))
        x_add.append(head_of(jnp.where(k < x, jnp.exp(late[0] - nm), 0.0)))
        x_m, x_d = nm, nd
    chip_carry_m = jnp.full((8, 128), LOW, F32)
    for k in range(nz):
        ahead = x_m + pre_d[k]
        cm_k = jnp.maximum(ahead, pre_m[k])
        chip_carry_m = jnp.where(z == k, cm_k, chip_carry_m)
        c_factor[0, k] = jnp.broadcast_to(head_of(jnp.exp(ahead - cm_k)), (8, DV))
        c_factor[1, k] = jnp.broadcast_to(head_of(jnp.exp(pre_m[k] - cm_k)), (8, DV))
    c_send[0] = jnp.zeros((slice_rows, DV), F32)

    second_m = jnp.maximum(chip_carry_m + d0, m0)
    from_chip = jnp.exp(chip_carry_m + d0 - second_m)
    from_first = jnp.exp(m0 - second_m)
    carry_m = jnp.where(is_first, chip_carry_m, second_m)
    own_a = head_of(jnp.where(is_first, 1.0, from_chip))
    own_b = head_of(jnp.where(is_first, 0.0, from_first))
    oth_a = head_of(jnp.where(is_first, from_chip, 1.0))
    oth_b = head_of(jnp.where(is_first, from_first, 0.0))

    for copy in rx:
        copy.wait()
    total = r_in[0].astype(F32) * x_add[0]
    for k in range(1, nx):
        total = total * x_keep[k] + r_in[k].astype(F32) * x_add[k]

    def carried(i):
        return (total * c_factor[0, i, 0:1] + c_send[i] * c_factor[1, i, 0:1]).astype(BF16)

    cz = {}
    for k in FAR_FIRST:
        to = lax.rem(z + k, nz)
        t_send[to] = carried(to)
        copy = remote(t_send.at[to], c_in.at[z], (cz_sem.at[0, k], cz_sem.at[1, k]), z_peer(k))
        copy.start()
        cz[k] = copy
    c_in[z] = carried(z)
    w_second(0)

    def p_copy(k):
        at = slice_of(lax.rem(z + nz - k, nz))
        return remote(p_send.at[at], carry.at[core, at], (p_sem.at[0, k], p_sem.at[1, k]), other)

    def p_arrival(k):
        at = slice_of(lax.rem(z + nz - k, nz))
        return remote(p_send.at[at], carry.at[1 - core, at], (p_sem.at[0, k], p_sem.at[1, k]), other)

    def spread(k):
        i = lax.rem(z + nz - k, nz)
        piece = c_in[i].astype(F32)
        first = jnp.where(is_first, state[slice_of(i), :], st_recv[slice_of(i), :].astype(F32))
        p_send[slice_of(i), :] = (piece * oth_a + first * oth_b).astype(BF16)
        carry[core, slice_of(i), :] = (piece * own_a + first * own_b).astype(BF16)
        p_copy(k).start()

    spread(0)
    for k in reversed(FAR_FIRST):
        cz[k].wait_recv()
        spread(k)
    for k in FAR_FIRST:
        cz[k].wait_send()
    loads[6].wait()
    loads[7].wait()
    loads[8].wait()
    w_third(0)
    for k in range(nz):
        p_copy(k).wait_send()
        p_arrival(k).wait_recv()

    def token(i):
        return pl.ds(pl.multiple_of(i * ROWS, ROWS), ROWS)

    def norm(i):
        at = token(i)
        column = cm_col[at, :]
        for h in range(2):
            gap = carry_m[h : h + 1, 0:1] - column[:, h : h + 1]
            top = jnp.maximum(gap, 0.0)
            total = local[h, at, :] * jnp.exp(-top) + jnp.exp(gap - top) * dot(q[h, at, :], carry[h])
            scale = lax.rsqrt(jnp.mean(total * total, axis=1, keepdims=True) + 1e-6)
            normed[at, h * DV : (h + 1) * DV] = (
                total * scale * gain[0:1, h * DV : (h + 1) * DV]
            ).astype(BF16)

    def ag_copy(i):
        return remote(normed.at[token(i)], normed_in.at[token(i)], (ag_sem.at[0, i], ag_sem.at[1, i]), me, pair)

    def rs_copy(i):
        return remote(part_s.at[i], part_r.at[i], (rs_sem.at[0, i], rs_sem.at[1, i]), me, mate)

    def out_copy(i):
        return pltpu.make_async_copy(out_v.at[token(i)], out_hbm.at[token(i)], out_sem.at[i])

    def each(lo, hi, fn):
        def step(i, _):
            fn(i)
            return 0

        lax.fori_loop(lo, hi, step, 0)

    def norm_and_send(i):
        norm(i)
        ag_copy(i).start()

    each(0, AHEAD, norm_and_send)
    each(AHEAD, PIECES, norm)

    def own(i):
        at = pl.ds(pl.multiple_of(lax.rem(i, 4) * 256, 256), 256)
        acc[lax.div(i, 4), :, at] = dot(normed[...], w[lax.div(i, 4), :, at])

    each(0, 8, own)
    w_second(1)
    w_wait(0)

    def finish(i):
        rs_copy(i).wait_recv()
        total = acc[1, token(i), :] + part_r[i].astype(F32)
        out_v[token(i), :] = total.astype(BF16)
        out_copy(i).start()

    def work(i):
        ag_copy(i).wait_recv()

        @pl.when(i + AHEAD < PIECES)
        def _():
            ag_copy(i).wait_send()
            ag_copy(i + AHEAD).start()

        far = normed_in[token(i), :]
        part_s[i] = (acc[0, token(i), :] + dot(far, w_far[0])).astype(BF16)
        rs_copy(i).start()

    each(0, LAG, work)

    def here(i):
        acc[1, token(i), :] = acc[1, token(i), :] + dot(normed_in[token(i), :], w_far[1])

    def both(i):
        work(i)
        here(i - LAG)
        finish(i - LAG)

    w_third(1)
    w_wait(1)
    each(LAG, PIECES, both)
    each(PIECES - LAG, PIECES, here)
    each(PIECES - LAG, PIECES, finish)

    def drain(i):
        rs_copy(i).wait_send()
        out_copy(i).wait()

    each(0, PIECES, drain)
    each(PIECES - AHEAD, PIECES, lambda i: ag_copy(i).wait_send())
    w_drain(0)
    w_drain(1)


def solution(mesh):
    nx, nz = NX, NZ
    slice_rows = DK // nz

    def body(conv_in, conv_weight, conv_bias, qk_weight, value_in, gate_pre, norm_gain, out_weight):
        dma = pltpu.SemaphoreType.DMA
        vmem = pltpu.VMEM
        return pl.pallas_call(
            body_kernel,
            out_shape=jax.ShapeDtypeStruct((T, COLS), BF16),
            in_specs=[pl.BlockSpec(memory_space=pl.ANY)] * 8,
            out_specs=pl.BlockSpec(memory_space=pl.ANY),
            scratch_shapes=[
                vmem((T, 2 * DK), BF16),
                vmem((4, 2 * DK), F32),
                vmem((1, 2 * DK), F32),
                vmem((2, 2, DK, DK), BF16),
                vmem((T, 2 * DV), BF16),
                vmem((2, 2, T), F32),
                vmem((1, 2 * DV), F32),
                vmem((2, 2 * DV, COLS), BF16),
                vmem((T + 8, 2 * DK), F32),
                vmem((16, 2 * DK), BF16),
                vmem((T, 2 * DK), BF16),
                vmem((2, T, DK), BF16),
                vmem((2, DK, T), BF16),
                vmem((DK, DV), F32),
                vmem((DK, DV), F32),
                vmem((2, T, DV), F32),
                vmem((16, 128), F32),
                vmem((16, 128), F32),
                vmem((nz, 16, 128), F32),
                vmem((nx, 16, 128), F32),
                vmem((DK, DV), BF16),
                vmem((DK, DV), BF16),
                vmem((nz, slice_rows, DV), BF16),
                vmem((nz, slice_rows, DV), BF16),
                vmem((slice_rows, DV), BF16),
                vmem((nx, slice_rows, DV), BF16),
                vmem((nz, slice_rows, DV), F32),
                vmem((2, nz, 8, DV), F32),
                vmem((nz, slice_rows, DV), BF16),
                vmem((DK, DV), BF16),
                vmem((2, DK, DV), BF16),
                vmem((T, 128), F32),
                vmem((T, 2 * DV), BF16),
                vmem((T, 2 * DV), BF16),
                vmem((2, T, COLS), F32),
                vmem((PIECES, ROWS, COLS), BF16),
                vmem((PIECES, ROWS, COLS), BF16),
                vmem((2, 2 * DV, COLS), BF16),
                vmem((T, COLS), BF16),
                dma((9,)),
                dma((2,)),
                dma((2,)),
                dma((2, nz)),
                dma((2, nx)),
                dma((2,)),
                dma((2, nz)),
                dma((2, nx)),
                dma((2, nz)),
                dma((2, nz)),
                dma((2, 2)),
                dma((2, 2, 2)),
                dma((2, 2, 2)),
                dma((2, 2, nx)),
                dma((2, PIECES)),
                dma((2, PIECES)),
                dma((PIECES,)),
            ],
            compiler_params=pltpu.CompilerParams(
                collective_id=0, has_side_effects=True, vmem_limit_bytes=56 * 1024 * 1024
            ),
        )(
            conv_in, conv_weight, conv_bias.reshape(1, -1), qk_weight, value_in, gate_pre,
            norm_gain.reshape(1, -1), out_weight,
        )

    return jax.shard_map(
        body,
        mesh=mesh,
        in_specs=(
            P("ctx", "head"),
            P(None, "head"),
            P("head"),
            P(None, "head", None, None),
            P("ctx", "head"),
            P(None, "head", "ctx"),
            P("head"),
            P("head", None),
        ),
        out_specs=P("ctx", "head"),
        check_vma=False,
    )
```

```python
import jax
import jax.numpy as jnp
from jax import lax
from jax.experimental import pallas as pl
from jax.experimental.pallas import tpu as pltpu
from jax.sharding import PartitionSpec as P

MESH = pl.DeviceIdType.MESH
F32 = jnp.float32
BF16 = jnp.bfloat16
LOW = -1e30

T = 512
HALF = 256
DK = 256
DV = 512
DM = 4096
FAR_FIRST = (4, 3, 5, 2, 6, 1, 7)
NX, NZ, NY = 4, 8, 4
COLS = DM // NY
ROWS = 64
PIECES = T // ROWS
LATE = 128
EDGE = 16
SMALL = 16
LAG = 3


def dot(a, b):
    return jnp.dot(a, b, preferred_element_type=F32)


def scan_lanes(v, combine, fill):
    lane = lax.broadcasted_iota(jnp.int32, v.shape, 1)
    shift = 1
    while shift < v.shape[1]:
        moved = pltpu.roll(v, shift, 1)
        v = combine(v, jnp.where(lane >= shift, moved, fill))
        shift *= 2
    return v


def join(early, late):
    return jnp.maximum(early[0] + late[1], late[0]), early[1] + late[1]


def body_kernel(
    conv_hbm, cw_hbm, cb_hbm, qk_hbm, val_hbm, gate_hbm, gain_hbm, w_hbm,
    out,
    conv_v, cw, cb, qk, val, gate, gain, w, xpad, halo, act, q, kt, state, state_oth, local,
    sc_own, sc_other, sc_chip, sc_row, st_send, st_recv, t_send, t_in, r_send, r_in,
    c_send, c_factor, c_in, p_send, carry, cm_col, normed, normed_in, acc, part_s, part_r, w_far,
    ld_sem, halo_sem, sc_sem, scz_sem, scx_sem, st_sem, tz_sem, rx_sem, cz_sem, p_sem,
    wy_sem, wx_sem, wh_sem, wc_sem, ag_sem, rs_sem,
):
    nx, nz = NX, NZ
    n_ctx = nx * nz * 2
    slice_rows = DK // nz
    me = lax.axis_index("ctx")
    y = lax.axis_index("head")
    core = lax.rem(me, 2)
    chip = lax.div(me, 2)
    z = lax.rem(chip, nz)
    x = lax.div(chip, nz)
    other = me + 1 - 2 * core

    def z_peer(k):
        return (x * nz + lax.rem(z + k, nz)) * 2 + core

    def x_peer(k):
        return (lax.rem(x + k, nx) * nz + z) * 2 + core

    pair = y + 1 - 2 * lax.rem(y, 2)
    mate = NY - 1 - y

    def remote(src, dst, sems, to, at_y=None):
        return pltpu.make_async_remote_copy(
            src_ref=src, dst_ref=dst, send_sem=sems[0], recv_sem=sems[1],
            device_id=(to, y if at_y is None else at_y), device_id_type=MESH,
        )

    loads = [
        pltpu.make_async_copy(src, dst, ld_sem.at[i])
        for i, (src, dst) in enumerate(
            [(gate_hbm, gate), (conv_hbm, conv_v), (cw_hbm, cw), (cb_hbm, cb),
             (qk_hbm, qk), (val_hbm, val), (gain_hbm, gain),
             (w_hbm.at[:, pl.ds(pl.multiple_of(mate * COLS, COLS), COLS)], w.at[0]),
             (w_hbm.at[:, pl.ds(pl.multiple_of(y * COLS, COLS), COLS)], w.at[1])]
        )
    ]
    for load in loads:
        load.start()

    barrier = pltpu.get_barrier_semaphore()
    after = lax.rem(me + 1, n_ctx)
    before = lax.rem(me + n_ctx - 1, n_ctx)
    greet = [(after, y), (before, y), (other, y)]
    greet += [(z_peer(k), y) for k in range(1, nz)]
    greet += [(x_peer(k), y) for k in range(1, nx)]
    greet += [(me, pair), (me, mate)]
    for to in greet:
        pl.semaphore_signal(barrier, inc=1, device_id=to, device_id_type=MESH)

    loads[0].wait()
    pad = jnp.zeros((6, T), F32)
    in_gate = jnp.concatenate([gate[0], pad], axis=0)
    forget = jnp.concatenate([gate[1], pad], axis=0)
    log_forget = jnp.minimum(forget, 0.0) - jnp.log1p(jnp.exp(-jnp.abs(forget)))
    cum = scan_lanes(log_forget, jnp.add, 0.0)
    g = in_gate - cum
    cm = scan_lanes(g, jnp.maximum, LOW)
    cum_end = cum[:, T - 1 :]
    cm_end = cm[:, T - 1 :]
    sc_own[0:8] = jnp.broadcast_to(cum_end + cm_end, (8, 128))
    sc_own[8:16] = jnp.broadcast_to(cum_end, (8, 128))
    cm_t = jnp.transpose(cm)
    cm_col[:, 0:8] = cm_t
    key_scale = jnp.exp(g - cm_end)

    pl.semaphore_wait(barrier, len(greet))
    halo_copy = remote(
        conv_hbm.at[pl.ds(T - 16, 16)], halo, (halo_sem.at[0], halo_sem.at[1]), after
    )
    halo_copy.start()
    sc_copy = remote(sc_own, sc_other, (sc_sem.at[0], sc_sem.at[1]), other)
    sc_copy.start()

    w_rows = 2 * DV // (2 * nx)

    def w_piece(j, at_x, lo=0, count=w_rows):
        row = pl.multiple_of((lax.rem(at_x + nx, nx) * 2 + core) * w_rows + lo, 16)
        return w_far.at[j, pl.ds(row, count), :]

    def wy_copy(j):
        column = pl.multiple_of((NY - 1 - pair if j == 0 else pair) * COLS, COLS)
        row = pl.multiple_of((x * 2 + core) * w_rows, w_rows)
        return remote(w_hbm.at[pl.ds(row, w_rows), pl.ds(column, COLS)], w_piece(j, x),
                      (wy_sem.at[0, j], wy_sem.at[1, j]), me, pair)

    def wx_copy(j, side):
        piece = w_piece(j, x)
        return remote(piece, piece, (wx_sem.at[0, j, side], wx_sem.at[1, j, side]), x_peer((1, nx - 1)[side]))

    def wh_copy(j, side):
        piece = w_piece(j, x + (-1, 1)[side], side * (w_rows // 2), w_rows // 2)
        return remote(piece, piece, (wh_sem.at[0, j, side], wh_sem.at[1, j, side]), x_peer((1, nx - 1)[side]))

    def wc_copy(j, k):
        piece = w_piece(j, x + k)
        return remote(piece, piece, (wc_sem.at[0, j, k], wc_sem.at[1, j, k]), other)

    def w_first(j):
        wy_copy(j).wait_recv()
        wx_copy(j, 0).start()
        wx_copy(j, 1).start()
        wc_copy(j, 0).start()
        if j == 0:
            wy_copy(1).start()

    def w_second(j):
        for side in range(2):
            wx_copy(j, side).wait_recv()
            wh_copy(j, side).start()
            wc_copy(j, (nx - 1, 1)[side]).start()

    def w_third(j):
        for side in range(2):
            wh_copy(j, side).wait_recv()
        wc_copy(j, 2).start()

    def w_wait(j):
        for k in range(nx):
            wc_copy(j, k).wait()

    def w_drain(j):
        wy_copy(j).wait_send()
        for side in range(2):
            wx_copy(j, side).wait_send()
            wh_copy(j, side).wait_send()

    wy_copy(0).start()

    loads[1].wait()
    loads[2].wait()
    loads[3].wait()
    rows = 64

    def widen(i, _):
        r = pl.multiple_of(i * rows, rows)
        xpad[pl.ds(r + 8, rows), :] = conv_v[pl.ds(r, rows), :].astype(F32)
        return 0

    lax.fori_loop(0, T // rows, widen, 0)

    def conv(r, n):
        ext = xpad[pl.ds(r, n + 8), :]
        pre = cb[0:1, :] + cw[0:1, :] * ext[5 : 5 + n]
        for j in range(1, 4):
            pre = pre + cw[j : j + 1, :] * ext[5 + j : 5 + j + n]
        act[pl.ds(r, n), :] = (pre / (1.0 + jnp.exp(-pre))).astype(BF16)

    def conv_step(i, _):
        conv(pl.multiple_of(i * rows, rows), rows)
        return 0

    conv(EDGE, rows - EDGE)
    lax.fori_loop(1, T // rows, conv_step, 0)

    loads[4].wait()
    loads[5].wait()

    def project(h, lo, hi):
        col = pl.multiple_of(h * DK, DK)
        a = act[lo:hi, pl.ds(col, DK)]
        q[h, lo:hi, :] = dot(a, qk[0, h]).astype(BF16)
        kt[h, :, lo:hi] = (
            lax.dot_general(qk[1, h], a, (((0,), (1,)), ((), ())), preferred_element_type=F32)
            * (1.0 / 16.0)
        ).astype(BF16)

    def block_state(h, scale, lo, hi):
        col = pl.multiple_of(h * DV, DV)
        scaled = (kt[h, :, lo:hi].astype(F32) * scale[:, lo:hi]).astype(BF16)
        return dot(scaled, val[lo:hi, pl.ds(col, DV)])

    is_first = core == 0
    scale_own = jnp.where(is_first, key_scale[0:1], key_scale[1:2])
    scale_oth = jnp.where(is_first, key_scale[1:2], key_scale[0:1])
    project(1 - core, LATE, T)
    state_oth[...] = block_state(1 - core, scale_oth, LATE, T)
    project(core, LATE, T)
    state[...] = block_state(core, scale_own, LATE, T)

    halo_copy.wait()
    edge = halo[...].astype(F32)[8:16]
    xpad[0:8, :] = jnp.where(me > 0, edge, 0.0)
    conv(0, EDGE)
    project(1 - core, 0, LATE)
    st_send[...] = (state_oth[...] + block_state(1 - core, scale_oth, 0, LATE)).astype(BF16)
    st_copy = remote(st_send, st_recv, (st_sem.at[0], st_sem.at[1]), other)
    st_copy.start()
    project(core, 0, LATE)
    state[...] = state[...] + block_state(core, scale_own, 0, LATE)

    sc_copy.wait()
    own_m, own_d = sc_own[0:8], sc_own[8:16]
    oth_m, oth_d = sc_other[0:8], sc_other[8:16]
    m0 = jnp.where(is_first, own_m, oth_m)
    d0 = jnp.where(is_first, own_d, oth_d)
    m1 = jnp.where(is_first, oth_m, own_m)
    d1 = jnp.where(is_first, oth_d, own_d)
    chip_m, chip_d = join((m0, d0), (m1, d1))
    mine = jnp.concatenate([chip_m, chip_d], axis=0)
    sc_chip[z] = mine
    scz = []
    for k in range(1, nz):
        copy = remote(sc_chip.at[z], sc_chip.at[z], (scz_sem.at[0, k], scz_sem.at[1, k]), z_peer(k))
        copy.start()
        scz.append(copy)

    def head_of(tile):
        row = jnp.where(is_first, tile[0:1], tile[1:2])
        return jnp.concatenate([row] * (DV // 128), axis=1)

    st_copy.wait()
    own_factor = jnp.where(is_first, jnp.exp(m0 + d1 - chip_m), jnp.exp(m1 - chip_m))
    oth_factor = jnp.where(is_first, jnp.exp(m1 - chip_m), jnp.exp(m0 + d1 - chip_m))
    own_factor, oth_factor = head_of(own_factor), head_of(oth_factor)

    def slice_of(i):
        return pl.ds(pl.multiple_of(i * slice_rows, slice_rows), slice_rows)

    def pack(i):
        mixed = state[slice_of(i), :] * own_factor + st_recv[slice_of(i), :].astype(F32) * oth_factor
        return mixed.astype(BF16)

    tz = []
    for k in FAR_FIRST:
        to = lax.rem(z + k, nz)
        t_send[to] = pack(to)
        copy = remote(t_send.at[to], t_in.at[z], (tz_sem.at[0, k], tz_sem.at[1, k]), z_peer(k))
        copy.start()
        tz.append(copy)
    t_in[z] = pack(z)
    w_first(0)

    for copy in scz:
        copy.wait()
    row_m, row_d = jnp.full((8, 128), LOW, F32), jnp.zeros((8, 128), F32)
    pre_m, pre_d = [], []
    for k in range(nz):
        pre_m.append(row_m)
        pre_d.append(row_d)
        row_m, row_d = join((row_m, row_d), (sc_chip[k, 0:8], sc_chip[k, 8:16]))
    sc_row[x] = jnp.concatenate([row_m, row_d], axis=0)
    scx = []
    for k in range(1, nx):
        copy = remote(sc_row.at[x], sc_row.at[x], (scx_sem.at[0, k], scx_sem.at[1, k]), x_peer(k))
        copy.start()
        scx.append(copy)

    def inner(h):
        for part in range(2):
            lo, hi = part * HALF, (part + 1) * HALF
            scores = dot(q[h, lo:hi, :], kt[h, :, 0:hi])
            row = lax.broadcasted_iota(jnp.int32, (HALF, hi), 0) + lo
            col = lax.broadcasted_iota(jnp.int32, (HALF, hi), 1)
            gap = jnp.where(row >= col, g[h : h + 1, 0:hi] - cm_t[lo:hi, h : h + 1], LOW)
            weights = (scores * jnp.exp(gap)).astype(BF16)
            local[h, lo:hi, :] = dot(weights, val[0:hi, h * DV : (h + 1) * DV])

    inner(0)
    inner(1)

    to_row = []
    m, d = jnp.full((8, 128), LOW, F32), jnp.zeros((8, 128), F32)
    for k in reversed(range(nz)):
        to_row.insert(0, head_of(jnp.exp(sc_chip[k, 0:8] + d - row_m)))
        d = d + sc_chip[k, 8:16]
    keep, add = [], []
    for k in range(nz - 1):
        keep.append(head_of(jnp.exp(pre_m[k] + sc_chip[k, 8:16] - pre_m[k + 1])))
        add.append(head_of(jnp.exp(sc_chip[k, 0:8] - pre_m[k + 1])))
    for copy in tz:
        copy.wait()
    row_sum = t_in[0].astype(F32) * to_row[0]
    for k in range(1, nz):
        row_sum = row_sum + t_in[k].astype(F32) * to_row[k]
    r_send[...] = row_sum.astype(BF16)
    rx = []
    for k in (2, 1, 3):
        copy = remote(r_send, r_in.at[x], (rx_sem.at[0, k], rx_sem.at[1, k]), x_peer(k))
        copy.start()
        rx.append(copy)
    r_in[x] = r_send[...]
    run = t_in[0].astype(F32) * add[0]
    c_send[1] = run
    for k in range(1, nz - 1):
        run = run * keep[k] + t_in[k].astype(F32) * add[k]
        c_send[k + 1] = run
    for copy in scx:
        copy.wait()
    x_m, x_d = jnp.full((8, 128), LOW, F32), jnp.zeros((8, 128), F32)
    x_keep, x_add = [], []
    for k in range(nx):
        late = (
            jnp.where(k < x, sc_row[k, 0:8], LOW),
            jnp.where(k < x, sc_row[k, 8:16], 0.0),
        )
        nm, nd = join((x_m, x_d), late)
        x_keep.append(head_of(jnp.exp(x_m + late[1] - nm)))
        x_add.append(head_of(jnp.where(k < x, jnp.exp(late[0] - nm), 0.0)))
        x_m, x_d = nm, nd
    chip_carry_m = jnp.full((8, 128), LOW, F32)
    for k in range(nz):
        ahead = x_m + pre_d[k]
        cm_k = jnp.maximum(ahead, pre_m[k])
        chip_carry_m = jnp.where(z == k, cm_k, chip_carry_m)
        c_factor[0, k] = jnp.broadcast_to(head_of(jnp.exp(ahead - cm_k)), (8, DV))
        c_factor[1, k] = jnp.broadcast_to(head_of(jnp.exp(pre_m[k] - cm_k)), (8, DV))
    c_send[0] = jnp.zeros((slice_rows, DV), F32)

    second_m = jnp.maximum(chip_carry_m + d0, m0)
    from_chip = jnp.exp(chip_carry_m + d0 - second_m)
    from_first = jnp.exp(m0 - second_m)
    carry_m = jnp.where(is_first, chip_carry_m, second_m)
    own_a = head_of(jnp.where(is_first, 1.0, from_chip))
    own_b = head_of(jnp.where(is_first, 0.0, from_first))
    oth_a = head_of(jnp.where(is_first, from_chip, 1.0))
    oth_b = head_of(jnp.where(is_first, from_first, 0.0))

    for copy in rx:
        copy.wait()
    total = r_in[0].astype(F32) * x_add[0]
    for k in range(1, nx):
        total = total * x_keep[k] + r_in[k].astype(F32) * x_add[k]

    def carried(i):
        return (total * c_factor[0, i, 0:1] + c_send[i] * c_factor[1, i, 0:1]).astype(BF16)

    cz = {}
    for k in FAR_FIRST:
        to = lax.rem(z + k, nz)
        t_send[to] = carried(to)
        copy = remote(t_send.at[to], c_in.at[z], (cz_sem.at[0, k], cz_sem.at[1, k]), z_peer(k))
        copy.start()
        cz[k] = copy
    c_in[z] = carried(z)
    w_second(0)
    w_first(1)

    def p_copy(k):
        at = slice_of(lax.rem(z + nz - k, nz))
        return remote(p_send.at[at], carry.at[core, at], (p_sem.at[0, k], p_sem.at[1, k]), other)

    def p_arrival(k):
        at = slice_of(lax.rem(z + nz - k, nz))
        return remote(p_send.at[at], carry.at[1 - core, at], (p_sem.at[0, k], p_sem.at[1, k]), other)

    def spread(k):
        i = lax.rem(z + nz - k, nz)
        piece = c_in[i].astype(F32)
        first = jnp.where(is_first, state[slice_of(i), :], st_recv[slice_of(i), :].astype(F32))
        p_send[slice_of(i), :] = (piece * oth_a + first * oth_b).astype(BF16)
        carry[core, slice_of(i), :] = (piece * own_a + first * own_b).astype(BF16)
        p_copy(k).start()

    spread(0)
    for k in reversed(FAR_FIRST):
        cz[k].wait_recv()
        spread(k)
    for k in FAR_FIRST:
        cz[k].wait_send()
    loads[6].wait()
    loads[7].wait()
    loads[8].wait()

    def token(i):
        return pl.ds(pl.multiple_of(i * ROWS, ROWS), ROWS)

    def norm(i, h):
        at = token(i)
        col = pl.ds(pl.multiple_of(h * DV, DV), DV)
        column = cm_col[at, :]
        gap = jnp.where(h == 0, carry_m[0:1, 0:1] - column[:, 0:1], carry_m[1:2, 0:1] - column[:, 1:2])
        top = jnp.maximum(gap, 0.0)
        total = local[h, at, :] * jnp.exp(-top) + jnp.exp(gap - top) * dot(q[h, at, :], carry[h])
        scale = lax.rsqrt(jnp.mean(total * total, axis=1, keepdims=True) + 1e-6)
        normed[at, col] = (total * scale * gain[0:1, col]).astype(BF16)

    def each(lo, hi, fn):
        def step(i, _):
            fn(i)
            return 0

        lax.fori_loop(lo, hi, step, 0)

    LAST = PIECES - 1
    first_a = (LAST + 1, pl.ds(0, SMALL))
    first_b = (0, pl.ds(SMALL, ROWS - SMALL))
    last_a = (LAST, pl.ds(LAST * ROWS, ROWS - SMALL))
    last_b = (LAST + 2, pl.ds(T - SMALL, SMALL))

    def ag_copy(slot, at):
        return remote(normed.at[at], normed_in.at[at], (ag_sem.at[0, slot], ag_sem.at[1, slot]), me, pair)

    def rs_copy(slot, at):
        return remote(part_s.at[at], part_r.at[at], (rs_sem.at[0, slot], rs_sem.at[1, slot]), me, mate)

    def own(side, lo, hi):
        def step(i):
            at = pl.ds(pl.multiple_of(i * 256, 256), 256)
            acc[side, lo:hi, at] = dot(normed[lo:hi, :], w[side, :, at])

        each(0, COLS // 256, step)

    def work(slot, at):
        ag_copy(slot, at).wait_recv()
        part_s[at, :] = (acc[0, at, :] + dot(normed_in[at, :], w_far[0])).astype(BF16)
        rs_copy(slot, at).start()

    def here(i):
        acc[1, token(i), :] = acc[1, token(i), :] + dot(normed_in[token(i), :], w_far[1])

    def add(i):
        out[token(i), :] = (acc[1, token(i), :] + part_r[token(i), :].astype(F32)).astype(BF16)

    each(0, PIECES, lambda i: norm(i, core))
    w_third(0)
    for k in range(nz):
        p_copy(k).wait_send()
        p_arrival(k).wait_recv()
    norm(0, 1 - core)
    ag_copy(*first_a).start()
    ag_copy(*first_b).start()
    norm(1, 1 - core)
    ag_copy(1, token(1)).start()
    norm(2, 1 - core)
    ag_copy(2, token(2)).start()
    own(0, 0, ROWS)
    w_wait(0)
    work(*first_a)
    each(3, PIECES, lambda i: norm(i, 1 - core))
    work(*first_b)
    own(0, ROWS, T)
    w_second(1)
    own(1, 0, T)

    def middle(i):
        ag_copy(i, token(i)).wait_send()

        @pl.when(i + 2 < LAST)
        def _():
            ag_copy(i + 2, token(i + 2)).start()

        @pl.when(i + 2 == LAST)
        def _():
            ag_copy(*last_a).start()

        @pl.when(i + 2 == LAST + 1)
        def _():
            ag_copy(*last_b).start()

        work(i, token(i))

    each(1, LAG, middle)
    w_third(1)
    w_wait(1)
    each(0, LAG - 1, here)
    rs_copy(*first_a).wait_recv()
    rs_copy(*first_b).wait_recv()
    add(0)

    def both(i):
        middle(i)
        here(i - 1)

        @pl.when(i > LAG)
        def _():
            rs_copy(i - LAG, token(i - LAG)).wait_recv()
            add(i - LAG)

    each(LAG, LAST, both)
    work(*last_a)
    here(LAST - 1)
    work(*last_b)
    here(LAST)
    for i in range(LAST - LAG, LAST):
        rs_copy(i, token(i)).wait_recv()
        add(i)
    rs_copy(*last_a).wait_recv()
    rs_copy(*last_b).wait_recv()
    add(LAST)

    for piece in (first_a, first_b, last_a, last_b):
        ag_copy(*piece).wait_send()
        rs_copy(*piece).wait_send()
    each(1, LAST, lambda i: rs_copy(i, token(i)).wait_send())
    w_drain(0)
    w_drain(1)


def solution(mesh):
    nx, nz = NX, NZ
    slice_rows = DK // nz

    def body(conv_in, conv_weight, conv_bias, qk_weight, value_in, gate_pre, norm_gain, out_weight):
        dma = pltpu.SemaphoreType.DMA
        vmem = pltpu.VMEM
        return pl.pallas_call(
            body_kernel,
            out_shape=vmem((T, COLS), BF16),
            in_specs=[pl.BlockSpec(memory_space=pl.ANY)] * 8,
            out_specs=pl.BlockSpec(memory_space=vmem),
            scratch_shapes=[
                vmem((T, 2 * DK), BF16),
                vmem((4, 2 * DK), F32),
                vmem((1, 2 * DK), F32),
                vmem((2, 2, DK, DK), BF16),
                vmem((T, 2 * DV), BF16),
                vmem((2, 2, T), F32),
                vmem((1, 2 * DV), F32),
                vmem((2, 2 * DV, COLS), BF16),
                vmem((T + 8, 2 * DK), F32),
                vmem((16, 2 * DK), BF16),
                vmem((T, 2 * DK), BF16),
                vmem((2, T, DK), BF16),
                vmem((2, DK, T), BF16),
                vmem((DK, DV), F32),
                vmem((DK, DV), F32),
                vmem((2, T, DV), F32),
                vmem((16, 128), F32),
                vmem((16, 128), F32),
                vmem((nz, 16, 128), F32),
                vmem((nx, 16, 128), F32),
                vmem((DK, DV), BF16),
                vmem((DK, DV), BF16),
                vmem((nz, slice_rows, DV), BF16),
                vmem((nz, slice_rows, DV), BF16),
                vmem((slice_rows, DV), BF16),
                vmem((nx, slice_rows, DV), BF16),
                vmem((nz, slice_rows, DV), F32),
                vmem((2, nz, 8, DV), F32),
                vmem((nz, slice_rows, DV), BF16),
                vmem((DK, DV), BF16),
                vmem((2, DK, DV), BF16),
                vmem((T, 128), F32),
                vmem((T, 2 * DV), BF16),
                vmem((T, 2 * DV), BF16),
                vmem((2, T, COLS), F32),
                vmem((T, COLS), BF16),
                vmem((T, COLS), BF16),
                vmem((2, 2 * DV, COLS), BF16),
                dma((9,)),
                dma((2,)),
                dma((2,)),
                dma((2, nz)),
                dma((2, nx)),
                dma((2,)),
                dma((2, nz)),
                dma((2, nx)),
                dma((2, nz)),
                dma((2, nz)),
                dma((2, 2)),
                dma((2, 2, 2)),
                dma((2, 2, 2)),
                dma((2, 2, nx)),
                dma((2, PIECES + 2)),
                dma((2, PIECES + 2)),
            ],
            compiler_params=pltpu.CompilerParams(
                collective_id=0, has_side_effects=True, vmem_limit_bytes=56 * 1024 * 1024
            ),
        )(
            conv_in, conv_weight, conv_bias.reshape(1, -1), qk_weight, value_in, gate_pre,
            norm_gain.reshape(1, -1), out_weight,
        )

    return jax.shard_map(
        body,
        mesh=mesh,
        in_specs=(
            P("ctx", "head"),
            P(None, "head"),
            P("head"),
            P(None, "head", None, None),
            P("ctx", "head"),
            P(None, "head", "ctx"),
            P("head"),
            P("head", None),
        ),
        out_specs=P("ctx", "head"),
        check_vma=False,
    )
```

```python
import jax
import jax.numpy as jnp
from jax import lax
from jax.experimental import pallas as pl
from jax.experimental.pallas import tpu as pltpu
from jax.sharding import PartitionSpec as P

MESH = pl.DeviceIdType.MESH
F32 = jnp.float32
BF16 = jnp.bfloat16
LOW = -1e30

T = 512
HALF = 256
DK = 256
DV = 512
DM = 4096
FAR_FIRST = (4, 3, 5, 2, 6, 1, 7)
NX, NZ, NY = 4, 8, 4
COLS = DM // NY
ROWS = 64
PIECES = T // ROWS
LATE = 128
EDGE = 16
SMALL = 16
LAG = 3


def dot(a, b):
    return jnp.dot(a, b, preferred_element_type=F32)


def scan_lanes(v, combine, fill):
    lane = lax.broadcasted_iota(jnp.int32, v.shape, 1)
    shift = 1
    while shift < v.shape[1]:
        moved = pltpu.roll(v, shift, 1)
        v = combine(v, jnp.where(lane >= shift, moved, fill))
        shift *= 2
    return v


def join(early, late):
    return jnp.maximum(early[0] + late[1], late[0]), early[1] + late[1]


def body_kernel(
    conv_hbm, cw_hbm, cb_hbm, qk_hbm, val_hbm, gate_hbm, gain_hbm, w_hbm,
    out,
    conv_v, cw, cb, qk, val, gate, gain, w, xpad, halo, act, q, kt, state, state_oth, local,
    sc_own, sc_other, sc_chip, sc_row, st_send, st_recv, t_send, t_in, r_send, r_in,
    c_send, c_factor, c_in, p_send, carry, cm_col, normed, normed_in, acc, part_s, part_r, w_far,
    ld_sem, halo_sem, sc_sem, scz_sem, scx_sem, st_sem, tz_sem, rx_sem, cz_sem, p_sem,
    wy_sem, wx_sem, wh_sem, wc_sem, ag_sem, rs_sem,
):
    nx, nz = NX, NZ
    n_ctx = nx * nz * 2
    slice_rows = DK // nz
    me = lax.axis_index("ctx")
    y = lax.axis_index("head")
    core = lax.rem(me, 2)
    chip = lax.div(me, 2)
    z = lax.rem(chip, nz)
    x = lax.div(chip, nz)
    other = me + 1 - 2 * core

    def z_peer(k):
        return (x * nz + lax.rem(z + k, nz)) * 2 + core

    def x_peer(k):
        return (lax.rem(x + k, nx) * nz + z) * 2 + core

    pair = y + 1 - 2 * lax.rem(y, 2)
    mate = NY - 1 - y

    def remote(src, dst, sems, to, at_y=None):
        return pltpu.make_async_remote_copy(
            src_ref=src, dst_ref=dst, send_sem=sems[0], recv_sem=sems[1],
            device_id=(to, y if at_y is None else at_y), device_id_type=MESH,
        )

    loads = [
        pltpu.make_async_copy(src, dst, ld_sem.at[i])
        for i, (src, dst) in enumerate(
            [(gate_hbm, gate), (conv_hbm, conv_v), (cw_hbm, cw), (cb_hbm, cb),
             (qk_hbm, qk), (val_hbm, val), (gain_hbm, gain),
             (w_hbm.at[:, pl.ds(pl.multiple_of(mate * COLS, COLS), COLS)], w.at[0]),
             (w_hbm.at[:, pl.ds(pl.multiple_of(y * COLS, COLS), COLS)], w.at[1])]
        )
    ]
    barrier = pltpu.get_barrier_semaphore()
    after = lax.rem(me + 1, n_ctx)
    before = lax.rem(me + n_ctx - 1, n_ctx)
    greet = [(after, y), (before, y), (other, y)]
    greet += [(z_peer(k), y) for k in range(1, nz)]
    greet += [(x_peer(k), y) for k in range(1, nx)]
    greet += [(me, pair), (me, mate)]
    for to in greet:
        pl.semaphore_signal(barrier, inc=1, device_id=to, device_id_type=MESH)
    for load in loads:
        load.start()

    loads[0].wait()
    pad = jnp.zeros((6, T), F32)
    in_gate = jnp.concatenate([gate[0], pad], axis=0)
    forget = jnp.concatenate([gate[1], pad], axis=0)
    log_forget = jnp.minimum(forget, 0.0) - jnp.log1p(jnp.exp(-jnp.abs(forget)))
    cum = scan_lanes(log_forget, jnp.add, 0.0)
    g = in_gate - cum
    cm = scan_lanes(g, jnp.maximum, LOW)
    cum_end = cum[:, T - 1 :]
    cm_end = cm[:, T - 1 :]
    sc_own[0:8] = jnp.broadcast_to(cum_end + cm_end, (8, 128))
    sc_own[8:16] = jnp.broadcast_to(cum_end, (8, 128))
    cm_t = jnp.transpose(cm)
    cm_col[:, 0:8] = cm_t
    key_scale = jnp.exp(g - cm_end)

    pl.semaphore_wait(barrier, len(greet))
    halo_copy = remote(
        conv_hbm.at[pl.ds(T - 16, 16)], halo, (halo_sem.at[0], halo_sem.at[1]), after
    )
    halo_copy.start()
    sc_copy = remote(sc_own, sc_other, (sc_sem.at[0], sc_sem.at[1]), other)
    sc_copy.start()

    w_rows = 2 * DV // (2 * nx)

    def w_piece(j, at_x, lo=0, count=w_rows):
        row = pl.multiple_of((lax.rem(at_x + nx, nx) * 2 + core) * w_rows + lo, 16)
        return w_far.at[j, pl.ds(row, count), :]

    def y_copy(j, at_x, sems):
        column = pl.multiple_of((NY - 1 - pair if j == 0 else pair) * COLS, COLS)
        row = pl.multiple_of((lax.rem(at_x, nx) * 2 + core) * w_rows, w_rows)
        return remote(w_hbm.at[pl.ds(row, w_rows), pl.ds(column, COLS)], w_piece(j, at_x), sems, me, pair)

    def wy_copy(j):
        return y_copy(j, x, (wy_sem.at[0, j], wy_sem.at[1, j]))

    def wh_copy(j):
        return y_copy(j, x + 2, (wh_sem.at[0, j], wh_sem.at[1, j]))

    def wx_copy(j, side):
        piece = w_piece(j, x)
        return remote(piece, piece, (wx_sem.at[0, j, side], wx_sem.at[1, j, side]), x_peer((1, nx - 1)[side]))

    def wc_copy(j, k):
        piece = w_piece(j, x + k)
        return remote(piece, piece, (wc_sem.at[0, j, k], wc_sem.at[1, j, k]), other)

    def w_first(j):
        wy_copy(j).wait_recv()
        wx_copy(j, 0).start()
        wx_copy(j, 1).start()
        wc_copy(j, 0).start()

    def w_second(j):
        for side in range(2):
            wx_copy(j, side).wait_recv()
            wc_copy(j, (nx - 1, 1)[side]).start()

    def w_third(j):
        wh_copy(j).wait_recv()
        wc_copy(j, 2).start()

    def w_wait(j):
        for k in range(nx):
            wc_copy(j, k).wait()

    def w_drain(j):
        wy_copy(j).wait_send()
        wh_copy(j).wait_send()
        for side in range(2):
            wx_copy(j, side).wait_send()

    wy_copy(0).start()

    loads[1].wait()
    loads[2].wait()
    loads[3].wait()
    rows = 64

    def widen(i, _):
        r = pl.multiple_of(i * rows, rows)
        xpad[pl.ds(r + 8, rows), :] = conv_v[pl.ds(r, rows), :].astype(F32)
        return 0

    lax.fori_loop(0, T // rows, widen, 0)

    def conv(r, n):
        ext = xpad[pl.ds(r, n + 8), :]
        pre = cb[0:1, :] + cw[0:1, :] * ext[5 : 5 + n]
        for j in range(1, 4):
            pre = pre + cw[j : j + 1, :] * ext[5 + j : 5 + j + n]
        act[pl.ds(r, n), :] = (pre / (1.0 + jnp.exp(-pre))).astype(BF16)

    def conv_step(i, _):
        conv(pl.multiple_of(i * rows, rows), rows)
        return 0

    conv(EDGE, rows - EDGE)
    lax.fori_loop(1, T // rows, conv_step, 0)

    loads[4].wait()
    loads[5].wait()

    def project(h, lo, hi):
        col = pl.multiple_of(h * DK, DK)
        a = act[lo:hi, pl.ds(col, DK)]
        q[h, lo:hi, :] = dot(a, qk[0, h]).astype(BF16)
        kt[h, :, lo:hi] = (
            lax.dot_general(qk[1, h], a, (((0,), (1,)), ((), ())), preferred_element_type=F32)
            * (1.0 / 16.0)
        ).astype(BF16)

    def block_state(h, scale, lo, hi):
        col = pl.multiple_of(h * DV, DV)
        scaled = (kt[h, :, lo:hi].astype(F32) * scale[:, lo:hi]).astype(BF16)
        return dot(scaled, val[lo:hi, pl.ds(col, DV)])

    is_first = core == 0
    scale_own = jnp.where(is_first, key_scale[0:1], key_scale[1:2])
    scale_oth = jnp.where(is_first, key_scale[1:2], key_scale[0:1])
    project(1 - core, LATE, T)
    state_oth[...] = block_state(1 - core, scale_oth, LATE, T)
    project(core, LATE, T)
    state[...] = block_state(core, scale_own, LATE, T)

    halo_copy.wait()
    edge = halo[...].astype(F32)[8:16]
    xpad[0:8, :] = jnp.where(me > 0, edge, 0.0)
    conv(0, EDGE)
    project(1 - core, 0, LATE)
    st_send[...] = (state_oth[...] + block_state(1 - core, scale_oth, 0, LATE)).astype(BF16)
    st_copy = remote(st_send, st_recv, (st_sem.at[0], st_sem.at[1]), other)
    st_copy.start()
    wh_copy(0).start()
    project(core, 0, LATE)
    state[...] = state[...] + block_state(core, scale_own, 0, LATE)

    sc_copy.wait()
    own_m, own_d = sc_own[0:8], sc_own[8:16]
    oth_m, oth_d = sc_other[0:8], sc_other[8:16]
    m0 = jnp.where(is_first, own_m, oth_m)
    d0 = jnp.where(is_first, own_d, oth_d)
    m1 = jnp.where(is_first, oth_m, own_m)
    d1 = jnp.where(is_first, oth_d, own_d)
    chip_m, chip_d = join((m0, d0), (m1, d1))
    mine = jnp.concatenate([chip_m, chip_d], axis=0)
    sc_chip[z] = mine
    scz = []
    for k in range(1, nz):
        copy = remote(sc_chip.at[z], sc_chip.at[z], (scz_sem.at[0, k], scz_sem.at[1, k]), z_peer(k))
        copy.start()
        scz.append(copy)

    def head_of(tile):
        row = jnp.where(is_first, tile[0:1], tile[1:2])
        return jnp.concatenate([row] * (DV // 128), axis=1)

    st_copy.wait()
    own_factor = jnp.where(is_first, jnp.exp(m0 + d1 - chip_m), jnp.exp(m1 - chip_m))
    oth_factor = jnp.where(is_first, jnp.exp(m1 - chip_m), jnp.exp(m0 + d1 - chip_m))
    own_factor, oth_factor = head_of(own_factor), head_of(oth_factor)

    def slice_of(i):
        return pl.ds(pl.multiple_of(i * slice_rows, slice_rows), slice_rows)

    def pack(i):
        mixed = state[slice_of(i), :] * own_factor + st_recv[slice_of(i), :].astype(F32) * oth_factor
        return mixed.astype(BF16)

    tz = []
    for k in FAR_FIRST:
        to = lax.rem(z + k, nz)
        t_send[to] = pack(to)
        copy = remote(t_send.at[to], t_in.at[z], (tz_sem.at[0, k], tz_sem.at[1, k]), z_peer(k))
        copy.start()
        tz.append(copy)
    t_in[z] = pack(z)
    w_first(0)

    for copy in scz:
        copy.wait()
    row_m, row_d = jnp.full((8, 128), LOW, F32), jnp.zeros((8, 128), F32)
    pre_m, pre_d = [], []
    for k in range(nz):
        pre_m.append(row_m)
        pre_d.append(row_d)
        row_m, row_d = join((row_m, row_d), (sc_chip[k, 0:8], sc_chip[k, 8:16]))
    sc_row[x] = jnp.concatenate([row_m, row_d], axis=0)
    scx = []
    for k in range(1, nx):
        copy = remote(sc_row.at[x], sc_row.at[x], (scx_sem.at[0, k], scx_sem.at[1, k]), x_peer(k))
        copy.start()
        scx.append(copy)

    def inner(h):
        for part in range(2):
            lo, hi = part * HALF, (part + 1) * HALF
            scores = dot(q[h, lo:hi, :], kt[h, :, 0:hi])
            row = lax.broadcasted_iota(jnp.int32, (HALF, hi), 0) + lo
            col = lax.broadcasted_iota(jnp.int32, (HALF, hi), 1)
            gap = jnp.where(row >= col, g[h : h + 1, 0:hi] - cm_t[lo:hi, h : h + 1], LOW)
            weights = (scores * jnp.exp(gap)).astype(BF16)
            local[h, lo:hi, :] = dot(weights, val[0:hi, h * DV : (h + 1) * DV])

    inner(0)
    inner(1)
    wy_copy(1).start()

    to_row = []
    m, d = jnp.full((8, 128), LOW, F32), jnp.zeros((8, 128), F32)
    for k in reversed(range(nz)):
        to_row.insert(0, head_of(jnp.exp(sc_chip[k, 0:8] + d - row_m)))
        d = d + sc_chip[k, 8:16]
    keep, add = [], []
    for k in range(nz - 1):
        keep.append(head_of(jnp.exp(pre_m[k] + sc_chip[k, 8:16] - pre_m[k + 1])))
        add.append(head_of(jnp.exp(sc_chip[k, 0:8] - pre_m[k + 1])))
    for copy in tz:
        copy.wait()
    row_sum = t_in[0].astype(F32) * to_row[0]
    for k in range(1, nz):
        row_sum = row_sum + t_in[k].astype(F32) * to_row[k]
    r_send[...] = row_sum.astype(BF16)
    rx = []
    for k in (2, 1, 3):
        copy = remote(r_send, r_in.at[x], (rx_sem.at[0, k], rx_sem.at[1, k]), x_peer(k))
        copy.start()
        rx.append(copy)
    r_in[x] = r_send[...]
    run = t_in[0].astype(F32) * add[0]
    c_send[1] = run
    for k in range(1, nz - 1):
        run = run * keep[k] + t_in[k].astype(F32) * add[k]
        c_send[k + 1] = run
    for copy in scx:
        copy.wait()
    x_m, x_d = jnp.full((8, 128), LOW, F32), jnp.zeros((8, 128), F32)
    x_keep, x_add = [], []
    for k in range(nx):
        late = (
            jnp.where(k < x, sc_row[k, 0:8], LOW),
            jnp.where(k < x, sc_row[k, 8:16], 0.0),
        )
        nm, nd = join((x_m, x_d), late)
        x_keep.append(head_of(jnp.exp(x_m + late[1] - nm)))
        x_add.append(head_of(jnp.where(k < x, jnp.exp(late[0] - nm), 0.0)))
        x_m, x_d = nm, nd
    chip_carry_m = jnp.full((8, 128), LOW, F32)
    for k in range(nz):
        ahead = x_m + pre_d[k]
        cm_k = jnp.maximum(ahead, pre_m[k])
        chip_carry_m = jnp.where(z == k, cm_k, chip_carry_m)
        c_factor[0, k] = jnp.broadcast_to(head_of(jnp.exp(ahead - cm_k)), (8, DV))
        c_factor[1, k] = jnp.broadcast_to(head_of(jnp.exp(pre_m[k] - cm_k)), (8, DV))
    c_send[0] = jnp.zeros((slice_rows, DV), F32)

    second_m = jnp.maximum(chip_carry_m + d0, m0)
    from_chip = jnp.exp(chip_carry_m + d0 - second_m)
    from_first = jnp.exp(m0 - second_m)
    carry_m = jnp.where(is_first, chip_carry_m, second_m)
    own_a = head_of(jnp.where(is_first, 1.0, from_chip))
    own_b = head_of(jnp.where(is_first, 0.0, from_first))
    oth_a = head_of(jnp.where(is_first, from_chip, 1.0))
    oth_b = head_of(jnp.where(is_first, from_first, 0.0))

    for copy in rx:
        copy.wait()
    total = r_in[0].astype(F32) * x_add[0]
    for k in range(1, nx):
        total = total * x_keep[k] + r_in[k].astype(F32) * x_add[k]

    def carried(i):
        return (total * c_factor[0, i, 0:1] + c_send[i] * c_factor[1, i, 0:1]).astype(BF16)

    cz = {}
    for k in FAR_FIRST:
        to = lax.rem(z + k, nz)
        t_send[to] = carried(to)
        copy = remote(t_send.at[to], c_in.at[z], (cz_sem.at[0, k], cz_sem.at[1, k]), z_peer(k))
        copy.start()
        cz[k] = copy
    c_in[z] = carried(z)
    w_second(0)
    w_third(0)
    w_first(1)
    wh_copy(1).start()

    def p_copy(k):
        at = slice_of(lax.rem(z + nz - k, nz))
        return remote(p_send.at[at], carry.at[core, at], (p_sem.at[0, k], p_sem.at[1, k]), other)

    def p_arrival(k):
        at = slice_of(lax.rem(z + nz - k, nz))
        return remote(p_send.at[at], carry.at[1 - core, at], (p_sem.at[0, k], p_sem.at[1, k]), other)

    def spread(k):
        i = lax.rem(z + nz - k, nz)
        piece = c_in[i].astype(F32)
        first = jnp.where(is_first, state[slice_of(i), :], st_recv[slice_of(i), :].astype(F32))
        p_send[slice_of(i), :] = (piece * oth_a + first * oth_b).astype(BF16)
        carry[core, slice_of(i), :] = (piece * own_a + first * own_b).astype(BF16)
        p_copy(k).start()

    spread(0)
    for k in reversed(FAR_FIRST):
        cz[k].wait_recv()
        spread(k)
    for k in FAR_FIRST:
        cz[k].wait_send()
    loads[6].wait()
    loads[7].wait()
    loads[8].wait()

    def token(i):
        return pl.ds(pl.multiple_of(i * ROWS, ROWS), ROWS)

    def norm(i, h):
        at = token(i)
        col = pl.ds(pl.multiple_of(h * DV, DV), DV)
        column = cm_col[at, :]
        gap = jnp.where(h == 0, carry_m[0:1, 0:1] - column[:, 0:1], carry_m[1:2, 0:1] - column[:, 1:2])
        top = jnp.maximum(gap, 0.0)
        total = local[h, at, :] * jnp.exp(-top) + jnp.exp(gap - top) * dot(q[h, at, :], carry[h])
        scale = lax.rsqrt(jnp.mean(total * total, axis=1, keepdims=True) + 1e-6)
        normed[at, col] = (total * scale * gain[0:1, col]).astype(BF16)

    def each(lo, hi, fn):
        def step(i, _):
            fn(i)
            return 0

        lax.fori_loop(lo, hi, step, 0)

    LAST = PIECES - 1
    first_a = (LAST + 1, pl.ds(0, SMALL))
    first_b = (0, pl.ds(SMALL, ROWS - SMALL))
    last_a = (LAST, pl.ds(LAST * ROWS, ROWS - SMALL))
    last_b = (LAST + 2, pl.ds(T - SMALL, SMALL))

    def ag_copy(slot, at):
        return remote(normed.at[at], normed_in.at[at], (ag_sem.at[0, slot], ag_sem.at[1, slot]), me, pair)

    def rs_copy(slot, at):
        return remote(part_s.at[at], part_r.at[at], (rs_sem.at[0, slot], rs_sem.at[1, slot]), me, mate)

    def own(side, lo, hi):
        def step(i):
            at = pl.ds(pl.multiple_of(i * 256, 256), 256)
            acc[side, lo:hi, at] = dot(normed[lo:hi, :], w[side, :, at])

        each(0, COLS // 256, step)

    def work(slot, at):
        ag_copy(slot, at).wait_recv()
        part_s[at, :] = (acc[0, at, :] + dot(normed_in[at, :], w_far[0])).astype(BF16)
        rs_copy(slot, at).start()

    def here(i):
        acc[1, token(i), :] = acc[1, token(i), :] + dot(normed_in[token(i), :], w_far[1])

    def add(i):
        out[token(i), :] = (acc[1, token(i), :] + part_r[token(i), :].astype(F32)).astype(BF16)

    each(0, PIECES, lambda i: norm(i, core))
    for k in range(nz):
        p_copy(k).wait_send()
        p_arrival(k).wait_recv()
    norm(0, 1 - core)
    ag_copy(*first_a).start()
    ag_copy(*first_b).start()
    norm(1, 1 - core)
    ag_copy(1, token(1)).start()
    norm(2, 1 - core)
    ag_copy(2, token(2)).start()
    own(0, 0, ROWS)
    each(3, PIECES, lambda i: norm(i, 1 - core))
    w_wait(0)
    work(*first_a)
    work(*first_b)
    own(0, ROWS, T)
    w_second(1)
    own(1, 0, T)

    def middle(i):
        ag_copy(i, token(i)).wait_send()

        @pl.when(i + 2 < LAST)
        def _():
            ag_copy(i + 2, token(i + 2)).start()

        @pl.when(i + 2 == LAST)
        def _():
            ag_copy(*last_a).start()

        @pl.when(i + 2 == LAST + 1)
        def _():
            ag_copy(*last_b).start()

        work(i, token(i))

    each(1, LAG, middle)
    w_third(1)
    w_wait(1)
    each(0, LAG - 1, here)
    rs_copy(*first_a).wait_recv()
    rs_copy(*first_b).wait_recv()
    add(0)

    def both(i):
        middle(i)
        here(i - 1)

        @pl.when(i > LAG)
        def _():
            rs_copy(i - LAG, token(i - LAG)).wait_recv()
            add(i - LAG)

    each(LAG, LAST, both)
    work(*last_a)
    here(LAST - 1)
    work(*last_b)
    here(LAST)
    for i in range(LAST - LAG, LAST):
        rs_copy(i, token(i)).wait_recv()
        add(i)
    rs_copy(*last_a).wait_recv()
    rs_copy(*last_b).wait_recv()
    add(LAST)

    for piece in (first_a, first_b, last_a, last_b):
        ag_copy(*piece).wait_send()
        rs_copy(*piece).wait_send()
    each(1, LAST, lambda i: rs_copy(i, token(i)).wait_send())
    w_drain(0)
    w_drain(1)


def solution(mesh):
    nx, nz = NX, NZ
    slice_rows = DK // nz

    def body(conv_in, conv_weight, conv_bias, qk_weight, value_in, gate_pre, norm_gain, out_weight):
        dma = pltpu.SemaphoreType.DMA
        vmem = pltpu.VMEM
        return pl.pallas_call(
            body_kernel,
            out_shape=vmem((T, COLS), BF16),
            in_specs=[pl.BlockSpec(memory_space=pl.ANY)] * 8,
            out_specs=pl.BlockSpec(memory_space=vmem),
            scratch_shapes=[
                vmem((T, 2 * DK), BF16),
                vmem((4, 2 * DK), F32),
                vmem((1, 2 * DK), F32),
                vmem((2, 2, DK, DK), BF16),
                vmem((T, 2 * DV), BF16),
                vmem((2, 2, T), F32),
                vmem((1, 2 * DV), F32),
                vmem((2, 2 * DV, COLS), BF16),
                vmem((T + 8, 2 * DK), F32),
                vmem((16, 2 * DK), BF16),
                vmem((T, 2 * DK), BF16),
                vmem((2, T, DK), BF16),
                vmem((2, DK, T), BF16),
                vmem((DK, DV), F32),
                vmem((DK, DV), F32),
                vmem((2, T, DV), F32),
                vmem((16, 128), F32),
                vmem((16, 128), F32),
                vmem((nz, 16, 128), F32),
                vmem((nx, 16, 128), F32),
                vmem((DK, DV), BF16),
                vmem((DK, DV), BF16),
                vmem((nz, slice_rows, DV), BF16),
                vmem((nz, slice_rows, DV), BF16),
                vmem((slice_rows, DV), BF16),
                vmem((nx, slice_rows, DV), BF16),
                vmem((nz, slice_rows, DV), F32),
                vmem((2, nz, 8, DV), F32),
                vmem((nz, slice_rows, DV), BF16),
                vmem((DK, DV), BF16),
                vmem((2, DK, DV), BF16),
                vmem((T, 128), F32),
                vmem((T, 2 * DV), BF16),
                vmem((T, 2 * DV), BF16),
                vmem((2, T, COLS), F32),
                vmem((T, COLS), BF16),
                vmem((T, COLS), BF16),
                vmem((2, 2 * DV, COLS), BF16),
                dma((9,)),
                dma((2,)),
                dma((2,)),
                dma((2, nz)),
                dma((2, nx)),
                dma((2,)),
                dma((2, nz)),
                dma((2, nx)),
                dma((2, nz)),
                dma((2, nz)),
                dma((2, 2)),
                dma((2, 2, 2)),
                dma((2, 2)),
                dma((2, 2, nx)),
                dma((2, PIECES + 2)),
                dma((2, PIECES + 2)),
            ],
            compiler_params=pltpu.CompilerParams(
                collective_id=0, has_side_effects=True, vmem_limit_bytes=56 * 1024 * 1024
            ),
        )(
            conv_in, conv_weight, conv_bias.reshape(1, -1), qk_weight, value_in, gate_pre,
            norm_gain.reshape(1, -1), out_weight,
        )

    return jax.shard_map(
        body,
        mesh=mesh,
        in_specs=(
            P("ctx", "head"),
            P(None, "head"),
            P("head"),
            P(None, "head", None, None),
            P("ctx", "head"),
            P(None, "head", "ctx"),
            P("head"),
            P("head", None),
        ),
        out_specs=P("ctx", "head"),
        check_vma=False,
    )
```

```python
import jax
import jax.numpy as jnp
from jax import lax
from jax.experimental import pallas as pl
from jax.experimental.pallas import tpu as pltpu
from jax.sharding import PartitionSpec as P

MESH = pl.DeviceIdType.MESH
F32 = jnp.float32
BF16 = jnp.bfloat16
LOW = -1e30

T = 512
HALF = 256
DK = 256
DV = 512
DM = 4096
FAR_FIRST = (4, 3, 5, 2, 6, 1, 7)
NX, NZ, NY = 4, 8, 4
COLS = DM // NY
ROWS = 64
PIECES = T // ROWS
LATE = 128
EDGE = 16
SMALL = 16
LAG = 3


def dot(a, b):
    return jnp.dot(a, b, preferred_element_type=F32)


def scan_lanes(v, combine, fill):
    lane = lax.broadcasted_iota(jnp.int32, v.shape, 1)
    shift = 1
    while shift < v.shape[1]:
        moved = pltpu.roll(v, shift, 1)
        v = combine(v, jnp.where(lane >= shift, moved, fill))
        shift *= 2
    return v


def join(early, late):
    return jnp.maximum(early[0] + late[1], late[0]), early[1] + late[1]


def body_kernel(
    conv_hbm, cw_hbm, cb_hbm, qk_hbm, val_hbm, gate_hbm, gain_hbm, w_hbm,
    out,
    conv_v, cw, cb, qk, val, gate, gain, w, xpad, halo, act, q, kt, state, state_oth, local,
    sc_own, sc_other, sc_chip, sc_row, st_send, st_recv, t_send, t_in, r_send, r_in,
    c_send, c_factor, c_in, p_send, carry, cm_col, normed, normed_in, acc, part_s, part_r, w_far,
    ld_sem, halo_sem, sc_sem, scz_sem, scx_sem, st_sem, tz_sem, rx_sem, cz_sem, p_sem,
    wy_sem, wx_sem, wh_sem, wc_sem, ag_sem, rs_sem,
):
    nx, nz = NX, NZ
    n_ctx = nx * nz * 2
    slice_rows = DK // nz
    me = lax.axis_index("ctx")
    y = lax.axis_index("head")
    core = lax.rem(me, 2)
    chip = lax.div(me, 2)
    z = lax.rem(chip, nz)
    x = lax.div(chip, nz)
    other = me + 1 - 2 * core

    def z_peer(k):
        return (x * nz + lax.rem(z + k, nz)) * 2 + core

    def x_peer(k):
        return (lax.rem(x + k, nx) * nz + z) * 2 + core

    pair = y + 1 - 2 * lax.rem(y, 2)
    mate = NY - 1 - y

    def remote(src, dst, sems, to, at_y=None):
        return pltpu.make_async_remote_copy(
            src_ref=src, dst_ref=dst, send_sem=sems[0], recv_sem=sems[1],
            device_id=(to, y if at_y is None else at_y), device_id_type=MESH,
        )

    loads = [
        pltpu.make_async_copy(src, dst, ld_sem.at[i])
        for i, (src, dst) in enumerate(
            [(gate_hbm, gate), (conv_hbm, conv_v), (cw_hbm, cw), (cb_hbm, cb),
             (qk_hbm, qk), (val_hbm, val), (gain_hbm, gain),
             (w_hbm.at[:, pl.ds(pl.multiple_of(mate * COLS, COLS), COLS)], w.at[0]),
             (w_hbm.at[:, pl.ds(pl.multiple_of(y * COLS, COLS), COLS)], w.at[1])]
        )
    ]
    barrier = pltpu.get_barrier_semaphore()
    after = lax.rem(me + 1, n_ctx)
    before = lax.rem(me + n_ctx - 1, n_ctx)
    greet = [(z_peer(k), y) for k in FAR_FIRST]
    greet += [(after, y), (before, y), (other, y)]
    greet += [(x_peer(k), y) for k in range(1, nx)]
    greet += [(me, pair), (me, mate)]
    for to in greet:
        pl.semaphore_signal(barrier, inc=1, device_id=to, device_id_type=MESH)
    for load in loads:
        load.start()

    loads[0].wait()
    pad = jnp.zeros((6, T), F32)
    in_gate = jnp.concatenate([gate[0], pad], axis=0)
    forget = jnp.concatenate([gate[1], pad], axis=0)
    log_forget = jnp.minimum(forget, 0.0) - jnp.log1p(jnp.exp(-jnp.abs(forget)))
    cum = scan_lanes(log_forget, jnp.add, 0.0)
    g = in_gate - cum
    cm = scan_lanes(g, jnp.maximum, LOW)
    cum_end = cum[:, T - 1 :]
    cm_end = cm[:, T - 1 :]
    sc_own[0:8] = jnp.broadcast_to(cum_end + cm_end, (8, 128))
    sc_own[8:16] = jnp.broadcast_to(cum_end, (8, 128))
    cm_t = jnp.transpose(cm)
    cm_col[:, 0:8] = cm_t
    key_scale = jnp.exp(g - cm_end)

    pl.semaphore_wait(barrier, len(greet))
    halo_copy = remote(
        conv_hbm.at[pl.ds(T - 16, 16)], halo, (halo_sem.at[0], halo_sem.at[1]), after
    )
    halo_copy.start()
    sc_copy = remote(sc_own, sc_other, (sc_sem.at[0], sc_sem.at[1]), other)
    sc_copy.start()

    w_rows = 2 * DV // (2 * nx)

    def w_piece(j, at_x, lo=0, count=w_rows):
        row = pl.multiple_of((lax.rem(at_x + nx, nx) * 2 + core) * w_rows + lo, 16)
        return w_far.at[j, pl.ds(row, count), :]

    def y_copy(j, at_x, sems):
        column = pl.multiple_of((NY - 1 - pair if j == 0 else pair) * COLS, COLS)
        row = pl.multiple_of((lax.rem(at_x, nx) * 2 + core) * w_rows, w_rows)
        return remote(w_hbm.at[pl.ds(row, w_rows), pl.ds(column, COLS)], w_piece(j, at_x), sems, me, pair)

    def wy_copy(j):
        return y_copy(j, x, (wy_sem.at[0, j], wy_sem.at[1, j]))

    def wh_copy(j):
        return y_copy(j, x + 2, (wh_sem.at[0, j], wh_sem.at[1, j]))

    def wx_copy(j, side):
        piece = w_piece(j, x)
        return remote(piece, piece, (wx_sem.at[0, j, side], wx_sem.at[1, j, side]), x_peer((1, nx - 1)[side]))

    def wc_copy(j, k):
        piece = w_piece(j, x + k)
        return remote(piece, piece, (wc_sem.at[0, j, k], wc_sem.at[1, j, k]), other)

    def w_first(j):
        wy_copy(j).wait_recv()
        wx_copy(j, 0).start()
        wx_copy(j, 1).start()
        wc_copy(j, 0).start()

    def w_second(j):
        for side in range(2):
            wx_copy(j, side).wait_recv()
            wc_copy(j, (nx - 1, 1)[side]).start()

    def w_third(j):
        wh_copy(j).wait_recv()
        wc_copy(j, 2).start()

    def w_wait(j):
        for k in range(nx):
            wc_copy(j, k).wait()

    def w_drain(j):
        wy_copy(j).wait_send()
        wh_copy(j).wait_send()
        for side in range(2):
            wx_copy(j, side).wait_send()

    wy_copy(0).start()

    loads[1].wait()
    loads[2].wait()
    loads[3].wait()
    rows = 64

    def widen(i, _):
        r = pl.multiple_of(i * rows, rows)
        xpad[pl.ds(r + 8, rows), :] = conv_v[pl.ds(r, rows), :].astype(F32)
        return 0

    lax.fori_loop(0, T // rows, widen, 0)

    def conv(r, n):
        ext = xpad[pl.ds(r, n + 8), :]
        pre = cb[0:1, :] + cw[0:1, :] * ext[5 : 5 + n]
        for j in range(1, 4):
            pre = pre + cw[j : j + 1, :] * ext[5 + j : 5 + j + n]
        act[pl.ds(r, n), :] = (pre / (1.0 + jnp.exp(-pre))).astype(BF16)

    def conv_step(i, _):
        conv(pl.multiple_of(i * rows, rows), rows)
        return 0

    conv(EDGE, rows - EDGE)
    lax.fori_loop(1, T // rows, conv_step, 0)

    loads[4].wait()
    loads[5].wait()

    def project(h, lo, hi):
        col = pl.multiple_of(h * DK, DK)
        a = act[lo:hi, pl.ds(col, DK)]
        q[h, lo:hi, :] = dot(a, qk[0, h]).astype(BF16)
        kt[h, :, lo:hi] = (
            lax.dot_general(qk[1, h], a, (((0,), (1,)), ((), ())), preferred_element_type=F32)
            * (1.0 / 16.0)
        ).astype(BF16)

    def block_state(h, scale, lo, hi):
        col = pl.multiple_of(h * DV, DV)
        scaled = (kt[h, :, lo:hi].astype(F32) * scale[:, lo:hi]).astype(BF16)
        return dot(scaled, val[lo:hi, pl.ds(col, DV)])

    is_first = core == 0
    scale_own = jnp.where(is_first, key_scale[0:1], key_scale[1:2])
    scale_oth = jnp.where(is_first, key_scale[1:2], key_scale[0:1])
    project(1 - core, LATE, T)
    state_oth[...] = block_state(1 - core, scale_oth, LATE, T)
    project(core, LATE, T)
    state[...] = block_state(core, scale_own, LATE, T)

    halo_copy.wait()
    edge = halo[...].astype(F32)[8:16]
    xpad[0:8, :] = jnp.where(me > 0, edge, 0.0)
    conv(0, EDGE)
    project(1 - core, 0, LATE)
    st_send[...] = (state_oth[...] + block_state(1 - core, scale_oth, 0, LATE)).astype(BF16)
    st_copy = remote(st_send, st_recv, (st_sem.at[0], st_sem.at[1]), other)
    st_copy.start()
    wh_copy(0).start()
    project(core, 0, LATE)
    state[...] = state[...] + block_state(core, scale_own, 0, LATE)

    sc_copy.wait()
    own_m, own_d = sc_own[0:8], sc_own[8:16]
    oth_m, oth_d = sc_other[0:8], sc_other[8:16]
    m0 = jnp.where(is_first, own_m, oth_m)
    d0 = jnp.where(is_first, own_d, oth_d)
    m1 = jnp.where(is_first, oth_m, own_m)
    d1 = jnp.where(is_first, oth_d, own_d)
    chip_m, chip_d = join((m0, d0), (m1, d1))
    mine = jnp.concatenate([chip_m, chip_d], axis=0)
    sc_chip[z] = mine
    scz = []
    for k in range(1, nz):
        copy = remote(sc_chip.at[z], sc_chip.at[z], (scz_sem.at[0, k], scz_sem.at[1, k]), z_peer(k))
        copy.start()
        scz.append(copy)

    def head_of(tile):
        row = jnp.where(is_first, tile[0:1], tile[1:2])
        return jnp.concatenate([row] * (DV // 128), axis=1)

    st_copy.wait()
    own_factor = jnp.where(is_first, jnp.exp(m0 + d1 - chip_m), jnp.exp(m1 - chip_m))
    oth_factor = jnp.where(is_first, jnp.exp(m1 - chip_m), jnp.exp(m0 + d1 - chip_m))
    own_factor, oth_factor = head_of(own_factor), head_of(oth_factor)

    def slice_of(i):
        return pl.ds(pl.multiple_of(i * slice_rows, slice_rows), slice_rows)

    def pack(i):
        mixed = state[slice_of(i), :] * own_factor + st_recv[slice_of(i), :].astype(F32) * oth_factor
        return mixed.astype(BF16)

    tz = []
    for k in FAR_FIRST:
        to = lax.rem(z + k, nz)
        t_send[to] = pack(to)
        copy = remote(t_send.at[to], t_in.at[z], (tz_sem.at[0, k], tz_sem.at[1, k]), z_peer(k))
        copy.start()
        tz.append(copy)
    t_in[z] = pack(z)
    w_first(0)

    for copy in scz:
        copy.wait()
    row_m, row_d = jnp.full((8, 128), LOW, F32), jnp.zeros((8, 128), F32)
    pre_m, pre_d = [], []
    for k in range(nz):
        pre_m.append(row_m)
        pre_d.append(row_d)
        row_m, row_d = join((row_m, row_d), (sc_chip[k, 0:8], sc_chip[k, 8:16]))
    sc_row[x] = jnp.concatenate([row_m, row_d], axis=0)
    scx = []
    for k in range(1, nx):
        copy = remote(sc_row.at[x], sc_row.at[x], (scx_sem.at[0, k], scx_sem.at[1, k]), x_peer(k))
        copy.start()
        scx.append(copy)

    def inner(h):
        for part in range(2):
            lo, hi = part * HALF, (part + 1) * HALF
            scores = dot(q[h, lo:hi, :], kt[h, :, 0:hi])
            row = lax.broadcasted_iota(jnp.int32, (HALF, hi), 0) + lo
            col = lax.broadcasted_iota(jnp.int32, (HALF, hi), 1)
            gap = jnp.where(row >= col, g[h : h + 1, 0:hi] - cm_t[lo:hi, h : h + 1], LOW)
            weights = (scores * jnp.exp(gap)).astype(BF16)
            local[h, lo:hi, :] = dot(weights, val[0:hi, h * DV : (h + 1) * DV])

    inner(0)
    inner(1)
    wy_copy(1).start()

    to_row = []
    m, d = jnp.full((8, 128), LOW, F32), jnp.zeros((8, 128), F32)
    for k in reversed(range(nz)):
        to_row.insert(0, head_of(jnp.exp(sc_chip[k, 0:8] + d - row_m)))
        d = d + sc_chip[k, 8:16]
    keep, add = [], []
    for k in range(nz - 1):
        keep.append(head_of(jnp.exp(pre_m[k] + sc_chip[k, 8:16] - pre_m[k + 1])))
        add.append(head_of(jnp.exp(sc_chip[k, 0:8] - pre_m[k + 1])))
    for copy in tz:
        copy.wait()
    row_sum = t_in[0].astype(F32) * to_row[0]
    for k in range(1, nz):
        row_sum = row_sum + t_in[k].astype(F32) * to_row[k]
    r_send[...] = row_sum.astype(BF16)
    rx = []
    for k in (2, 1, 3):
        copy = remote(r_send, r_in.at[x], (rx_sem.at[0, k], rx_sem.at[1, k]), x_peer(k))
        copy.start()
        rx.append(copy)
    r_in[x] = r_send[...]
    run = t_in[0].astype(F32) * add[0]
    c_send[1] = run
    for k in range(1, nz - 1):
        run = run * keep[k] + t_in[k].astype(F32) * add[k]
        c_send[k + 1] = run
    for copy in scx:
        copy.wait()
    x_m, x_d = jnp.full((8, 128), LOW, F32), jnp.zeros((8, 128), F32)
    x_keep, x_add = [], []
    for k in range(nx):
        late = (
            jnp.where(k < x, sc_row[k, 0:8], LOW),
            jnp.where(k < x, sc_row[k, 8:16], 0.0),
        )
        nm, nd = join((x_m, x_d), late)
        x_keep.append(head_of(jnp.exp(x_m + late[1] - nm)))
        x_add.append(head_of(jnp.where(k < x, jnp.exp(late[0] - nm), 0.0)))
        x_m, x_d = nm, nd
    chip_carry_m = jnp.full((8, 128), LOW, F32)
    for k in range(nz):
        ahead = x_m + pre_d[k]
        cm_k = jnp.maximum(ahead, pre_m[k])
        chip_carry_m = jnp.where(z == k, cm_k, chip_carry_m)
        c_factor[0, k] = jnp.broadcast_to(head_of(jnp.exp(ahead - cm_k)), (8, DV))
        c_factor[1, k] = jnp.broadcast_to(head_of(jnp.exp(pre_m[k] - cm_k)), (8, DV))
    c_send[0] = jnp.zeros((slice_rows, DV), F32)

    second_m = jnp.maximum(chip_carry_m + d0, m0)
    from_chip = jnp.exp(chip_carry_m + d0 - second_m)
    from_first = jnp.exp(m0 - second_m)
    carry_m = jnp.where(is_first, chip_carry_m, second_m)
    own_a = head_of(jnp.where(is_first, 1.0, from_chip))
    own_b = head_of(jnp.where(is_first, 0.0, from_first))
    oth_a = head_of(jnp.where(is_first, from_chip, 1.0))
    oth_b = head_of(jnp.where(is_first, from_first, 0.0))

    for copy in rx:
        copy.wait()
    total = r_in[0].astype(F32) * x_add[0]
    for k in range(1, nx):
        total = total * x_keep[k] + r_in[k].astype(F32) * x_add[k]

    def carried(i):
        return (total * c_factor[0, i, 0:1] + c_send[i] * c_factor[1, i, 0:1]).astype(BF16)

    cz = {}
    for k in FAR_FIRST:
        to = lax.rem(z + k, nz)
        t_send[to] = carried(to)
        copy = remote(t_send.at[to], c_in.at[z], (cz_sem.at[0, k], cz_sem.at[1, k]), z_peer(k))
        copy.start()
        cz[k] = copy
    c_in[z] = carried(z)
    w_second(0)
    w_third(0)
    w_first(1)
    wh_copy(1).start()

    def p_copy(k):
        at = slice_of(lax.rem(z + nz - k, nz))
        return remote(p_send.at[at], carry.at[core, at], (p_sem.at[0, k], p_sem.at[1, k]), other)

    def p_arrival(k):
        at = slice_of(lax.rem(z + nz - k, nz))
        return remote(p_send.at[at], carry.at[1 - core, at], (p_sem.at[0, k], p_sem.at[1, k]), other)

    def spread(k):
        i = lax.rem(z + nz - k, nz)
        piece = c_in[i].astype(F32)
        first = jnp.where(is_first, state[slice_of(i), :], st_recv[slice_of(i), :].astype(F32))
        p_send[slice_of(i), :] = (piece * oth_a + first * oth_b).astype(BF16)
        carry[core, slice_of(i), :] = (piece * own_a + first * own_b).astype(BF16)
        p_copy(k).start()

    spread(0)
    for k in reversed(FAR_FIRST):
        cz[k].wait_recv()
        spread(k)
    for k in FAR_FIRST:
        cz[k].wait_send()
    loads[6].wait()
    loads[7].wait()
    loads[8].wait()

    def token(i):
        return pl.ds(pl.multiple_of(i * ROWS, ROWS), ROWS)

    def norm(i, h):
        at = token(i)
        col = pl.ds(pl.multiple_of(h * DV, DV), DV)
        column = cm_col[at, :]
        gap = jnp.where(h == 0, carry_m[0:1, 0:1] - column[:, 0:1], carry_m[1:2, 0:1] - column[:, 1:2])
        top = jnp.maximum(gap, 0.0)
        total = local[h, at, :] * jnp.exp(-top) + jnp.exp(gap - top) * dot(q[h, at, :], carry[h])
        scale = lax.rsqrt(jnp.mean(total * total, axis=1, keepdims=True) + 1e-6)
        normed[at, col] = (total * scale * gain[0:1, col]).astype(BF16)

    def each(lo, hi, fn):
        def step(i, _):
            fn(i)
            return 0

        lax.fori_loop(lo, hi, step, 0)

    LAST = PIECES - 1
    first_a = (LAST + 1, pl.ds(0, SMALL))
    first_b = (0, pl.ds(SMALL, ROWS - SMALL))
    last_a = (LAST, pl.ds(LAST * ROWS, ROWS - SMALL))
    last_b = (LAST + 2, pl.ds(T - SMALL, SMALL))

    def ag_copy(slot, at):
        return remote(normed.at[at], normed_in.at[at], (ag_sem.at[0, slot], ag_sem.at[1, slot]), me, pair)

    def rs_copy(slot, at):
        return remote(part_s.at[at], part_r.at[at], (rs_sem.at[0, slot], rs_sem.at[1, slot]), me, mate)

    def own(side, lo, hi):
        def step(i):
            at = pl.ds(pl.multiple_of(i * 256, 256), 256)
            acc[side, lo:hi, at] = dot(normed[lo:hi, :], w[side, :, at])

        each(0, COLS // 256, step)

    def work(slot, at):
        ag_copy(slot, at).wait_recv()
        part_s[at, :] = (acc[0, at, :] + dot(normed_in[at, :], w_far[0])).astype(BF16)
        rs_copy(slot, at).start()

    def here(i):
        acc[1, token(i), :] = acc[1, token(i), :] + dot(normed_in[token(i), :], w_far[1])

    def add(i):
        out[token(i), :] = (acc[1, token(i), :] + part_r[token(i), :].astype(F32)).astype(BF16)

    each(0, PIECES, lambda i: norm(i, core))
    for k in range(nz):
        p_copy(k).wait_send()
        p_arrival(k).wait_recv()
    norm(0, 1 - core)
    ag_copy(*first_a).start()
    ag_copy(*first_b).start()
    norm(1, 1 - core)
    ag_copy(1, token(1)).start()
    norm(2, 1 - core)
    ag_copy(2, token(2)).start()
    own(0, 0, ROWS)
    each(3, PIECES, lambda i: norm(i, 1 - core))
    w_wait(0)
    work(*first_a)
    work(*first_b)
    own(0, ROWS, T)
    w_second(1)

    def middle(i):
        ag_copy(i, token(i)).wait_send()

        @pl.when(i + 2 < LAST)
        def _():
            ag_copy(i + 2, token(i + 2)).start()

        @pl.when(i + 2 == LAST)
        def _():
            ag_copy(*last_a).start()

        @pl.when(i + 2 == LAST + 1)
        def _():
            ag_copy(*last_b).start()

        work(i, token(i))

    middle(1)
    own(1, 0, HALF)
    each(2, LAG, middle)
    own(1, HALF, T)
    w_third(1)
    w_wait(1)
    each(0, LAG - 1, here)
    rs_copy(*first_a).wait_recv()
    rs_copy(*first_b).wait_recv()
    add(0)

    def both(i):
        middle(i)
        here(i - 1)

        @pl.when(i > LAG)
        def _():
            rs_copy(i - LAG, token(i - LAG)).wait_recv()
            add(i - LAG)

    each(LAG, LAST, both)
    work(*last_a)
    here(LAST - 1)
    work(*last_b)
    here(LAST)
    for i in range(LAST - LAG, LAST):
        rs_copy(i, token(i)).wait_recv()
        add(i)
    rs_copy(*last_a).wait_recv()
    rs_copy(*last_b).wait_recv()
    add(LAST)

    for piece in (first_a, first_b, last_a, last_b):
        ag_copy(*piece).wait_send()
        rs_copy(*piece).wait_send()
    each(1, LAST, lambda i: rs_copy(i, token(i)).wait_send())
    w_drain(0)
    w_drain(1)


def solution(mesh):
    nx, nz = NX, NZ
    slice_rows = DK // nz

    def body(conv_in, conv_weight, conv_bias, qk_weight, value_in, gate_pre, norm_gain, out_weight):
        dma = pltpu.SemaphoreType.DMA
        vmem = pltpu.VMEM
        return pl.pallas_call(
            body_kernel,
            out_shape=vmem((T, COLS), BF16),
            in_specs=[pl.BlockSpec(memory_space=pl.ANY)] * 8,
            out_specs=pl.BlockSpec(memory_space=vmem),
            scratch_shapes=[
                vmem((T, 2 * DK), BF16),
                vmem((4, 2 * DK), F32),
                vmem((1, 2 * DK), F32),
                vmem((2, 2, DK, DK), BF16),
                vmem((T, 2 * DV), BF16),
                vmem((2, 2, T), F32),
                vmem((1, 2 * DV), F32),
                vmem((2, 2 * DV, COLS), BF16),
                vmem((T + 8, 2 * DK), F32),
                vmem((16, 2 * DK), BF16),
                vmem((T, 2 * DK), BF16),
                vmem((2, T, DK), BF16),
                vmem((2, DK, T), BF16),
                vmem((DK, DV), F32),
                vmem((DK, DV), F32),
                vmem((2, T, DV), F32),
                vmem((16, 128), F32),
                vmem((16, 128), F32),
                vmem((nz, 16, 128), F32),
                vmem((nx, 16, 128), F32),
                vmem((DK, DV), BF16),
                vmem((DK, DV), BF16),
                vmem((nz, slice_rows, DV), BF16),
                vmem((nz, slice_rows, DV), BF16),
                vmem((slice_rows, DV), BF16),
                vmem((nx, slice_rows, DV), BF16),
                vmem((nz, slice_rows, DV), F32),
                vmem((2, nz, 8, DV), F32),
                vmem((nz, slice_rows, DV), BF16),
                vmem((DK, DV), BF16),
                vmem((2, DK, DV), BF16),
                vmem((T, 128), F32),
                vmem((T, 2 * DV), BF16),
                vmem((T, 2 * DV), BF16),
                vmem((2, T, COLS), F32),
                vmem((T, COLS), BF16),
                vmem((T, COLS), BF16),
                vmem((2, 2 * DV, COLS), BF16),
                dma((9,)),
                dma((2,)),
                dma((2,)),
                dma((2, nz)),
                dma((2, nx)),
                dma((2,)),
                dma((2, nz)),
                dma((2, nx)),
                dma((2, nz)),
                dma((2, nz)),
                dma((2, 2)),
                dma((2, 2, 2)),
                dma((2, 2)),
                dma((2, 2, nx)),
                dma((2, PIECES + 2)),
                dma((2, PIECES + 2)),
            ],
            compiler_params=pltpu.CompilerParams(
                collective_id=0, has_side_effects=True, vmem_limit_bytes=56 * 1024 * 1024
            ),
        )(
            conv_in, conv_weight, conv_bias.reshape(1, -1), qk_weight, value_in, gate_pre,
            norm_gain.reshape(1, -1), out_weight,
        )

    return jax.shard_map(
        body,
        mesh=mesh,
        in_specs=(
            P("ctx", "head"),
            P(None, "head"),
            P("head"),
            P(None, "head", None, None),
            P("ctx", "head"),
            P(None, "head", "ctx"),
            P("head"),
            P("head", None),
        ),
        out_specs=P("ctx", "head"),
        check_vma=False,
    )
```
